128 devices in a mesh: blk: 8 (over y_lo, x), dp: 16 (over y_hi, z, core).
Axes of the slice: x: 4, y: 4 (y_hi: 2, y_lo: 2; y = y_hi * 2 + y_lo), z: 4, core: 2. Of those that a mesh axis runs over, the one named last changes fastest.
Arguments:
- tokens: bfloat16 [32768, 5120], P(('blk', 'dp')), may hold values from -6 to 6
- cotangent: bfloat16 [32768, 5120], P(('blk', 'dp')), may hold values from -6 to 6
- in_weight: bfloat16 [5120, 896], P(('blk', 'dp')), may hold values from -1 to 1
- out_weight: bfloat16 [5120, 640], P(('blk', 'dp')), may hold values from -0.25 to 0.25
- norm_gain: bfloat16 [5120], P(('blk', 'dp')), may hold values from 0.099609375 to 1.8984375
Outputs:
- layer_out: bfloat16 [32768, 5120], P(('blk', 'dp'))
- input_grad: bfloat16 [32768, 5120], P(('blk', 'dp'))
- in_grad: float32 [5120, 896], P(('blk', 'dp'))
- out_grad: float32 [5120, 640], P(('blk', 'dp'))
- gain_grad: float32 [5120], P(('blk', 'dp'))
The draws below stay inside these ranges and needn't reach their ends.
All inputs are finite; a program needn't handle non-finite values.
Results may differ from the reference program's by a relative error of at most 0.029.
The reference program's roundings to bfloat16 on the way (of `normed`, `projected`, `weights_b`, `context`, `d_context`, `d_scores` and `d_proj`) count: a program that leaves them out, or rounds other values in their place, can miss the bound.
Values may be sent and summed in bfloat16 or wider, within the bound.
No kernel may reach another device: no remote copies, remote signals or barrier semaphores. Data moves between devices by JAX's collectives and lax.ppermute only.
A program may use at most 128 MiB of HBM per device.

```python
import math
import jax
import jax.numpy as jnp
from jax import lax

D = 5120
HEAD_DIM = 128
HEADS = 5
TOK_DEV = 256
TOKENS = 32768
N_BLK = 8
N_DP = 16


def draw_in_weight(key, part):
    key = jax.random.fold_in(key, 11)
    columns = (HEADS + 2) * HEAD_DIM
    base = jax.random.normal(key, (D, columns), jnp.float32) / math.sqrt(D)
    return jnp.clip(base, -1.0, 1.0).astype(jnp.bfloat16)


def level_of(own_key, dims, shards, smallest, top_value):
    def one(position, blocks):
        steps = jax.random.uniform(jax.random.fold_in(jax.random.fold_in(own_key, 6), position), (blocks,), jnp.float32, smallest / len(shards), top_value / len(shards))
        return jnp.repeat(jnp.exp(steps), dims[position] // blocks).reshape((-1,) + (1,) * (len(dims) - position - 1))

    level = one(*shards[0])
    for cut in shards[1:]:
        level = level * one(*cut)
    return level


def scatter_about(key, extent, spread, bound, cuts=(), held_as=jnp.bfloat16):
    factor_of = level_of(key, extent, cuts, -0.22, 0.18) if cuts else 1.0
    entries = jax.random.normal(key, extent, jnp.float32) * spread * factor_of
    return jnp.minimum(jnp.maximum(entries, -bound), bound).astype(held_as)


def setup_inputs(seed: int = 0) -> dict:
    keys = jax.random.split(jax.random.key(seed), 6)
    tokens = scatter_about(keys[0], (TOKENS, D), 1.0, 6.0, ((0, 128),))
    cotangent = scatter_about(keys[1], (TOKENS, D), 1.0, 6.0, ((0, 128),))
    in_weight = draw_in_weight(jax.random.fold_in(keys[5], 71), 0)
    out_weight = scatter_about(keys[3], (D, HEADS * HEAD_DIM), (HEADS * HEAD_DIM) ** -0.5, 0.25, ((0, 128),))
    norm_gain = jnp.clip(1.0 + 0.18 * jax.random.normal(keys[4], (D,), jnp.float32), 0.099609375, 1.8984375).astype(jnp.bfloat16)
    return {"tokens": tokens, "cotangent": cotangent, "in_weight": in_weight, "out_weight": out_weight, "norm_gain": norm_gain}


EPS = 1e-06

def one_sequence(tokens, cotangent, in_weight, out_weight, norm_gain):
    f32 = jnp.float32
    bf16 = jnp.bfloat16
    x_full = tokens.astype(f32)
    rscale = lax.rsqrt(lax.optimization_barrier(jnp.mean(x_full * x_full, axis=1, keepdims=True)) + EPS)
    scaled = x_full * rscale
    gain_f = norm_gain.astype(f32)
    normed = (scaled * gain_f[None, :]).astype(bf16)
    projected = jnp.dot(normed, in_weight, preferred_element_type=f32).astype(bf16)
    length = projected.shape[0]
    qwidth = HEADS * HEAD_DIM
    queries = projected[:, :qwidth].reshape(length, HEADS, HEAD_DIM).astype(f32)
    key_rows = projected[:, qwidth:qwidth + HEAD_DIM].astype(f32)
    value_rows = projected[:, qwidth + HEAD_DIM:].astype(f32)
    factor = 1.0 / math.sqrt(HEAD_DIM)
    scores = jnp.einsum('thd,sd->hts', queries, key_rows) * factor
    causal = lax.broadcasted_iota(jnp.int32, (length, length), 0) >= lax.broadcasted_iota(jnp.int32, (length, length), 1)
    scores = jnp.where(causal[None], scores, -jnp.inf)
    top_score = lax.optimization_barrier(jnp.max(scores, axis=2, keepdims=True))
    shifted = jnp.exp(scores - top_score)
    weights_f = shifted / lax.optimization_barrier(jnp.sum(shifted, axis=2, keepdims=True))
    weights_b = weights_f.astype(bf16)
    context = jnp.einsum('hts,sd->thd', weights_b.astype(f32), value_rows).reshape(length, qwidth).astype(bf16)
    attn_out = lax.dot_general(context, out_weight, (((1,), (1,)), ((), ())), preferred_element_type=f32)
    layer_out = (x_full + attn_out).astype(bf16)
    d_context = jnp.dot(cotangent, out_weight, preferred_element_type=f32).astype(bf16)
    d_heads = d_context.reshape(length, HEADS, HEAD_DIM).astype(f32)
    d_weights = jnp.einsum('thd,sd->hts', d_heads, value_rows)
    row_dot = lax.optimization_barrier(jnp.sum(weights_f * d_weights, axis=2, keepdims=True))
    d_scores = (weights_f * (d_weights - row_dot)).astype(bf16).astype(f32)
    d_queries = jnp.einsum('hts,sd->thd', d_scores, key_rows) * factor
    d_keys = jnp.einsum('hts,thd->sd', d_scores, queries) * factor
    d_values = jnp.einsum('hts,thd->sd', weights_b.astype(f32), d_heads)
    d_proj = jnp.concatenate([d_queries.reshape(length, qwidth), d_keys, d_values], axis=1).astype(bf16)
    d_normed = lax.dot_general(d_proj, in_weight, (((1,), (1,)), ((), ())), preferred_element_type=f32)
    gain_term = lax.optimization_barrier(jnp.sum(d_normed * scaled, axis=0))
    inner_mean = lax.optimization_barrier(jnp.mean(scaled * gain_f[None, :] * d_normed, axis=1, keepdims=True))
    input_grad = (cotangent.astype(f32) + rscale * (gain_f[None, :] * d_normed - scaled * inner_mean)).astype(bf16)
    in_term = lax.dot_general(normed, d_proj, (((0,), (0,)), ((), ())), preferred_element_type=f32)
    out_term = lax.dot_general(cotangent, context, (((0,), (0,)), ((), ())), preferred_element_type=f32)
    return (layer_out, input_grad, in_term, out_term, gain_term)

def rounded(value):
    return lax.optimization_barrier(value.astype(jnp.bfloat16)).astype(jnp.float32)

def reference(tokens, cotangent, in_weight, out_weight, norm_gain):
    seq_count = N_BLK * N_DP
    tok_seq = tokens.reshape(seq_count, TOK_DEV, D)
    cot_seq = cotangent.reshape(seq_count, TOK_DEV, D)

    def advance(totals, sequence):
        layer_out, input_grad, in_term, out_term, gain_term = one_sequence(sequence[0], sequence[1], in_weight, out_weight, norm_gain)
        totals = (totals[0] + rounded(in_term), totals[1] + rounded(out_term), totals[2] + rounded(gain_term))
        return (totals, (layer_out, input_grad))
    initial = (jnp.zeros(in_weight.shape, jnp.float32), jnp.zeros(out_weight.shape, jnp.float32), jnp.zeros(norm_gain.shape, jnp.float32))
    totals, stacked = lax.scan(advance, initial, (tok_seq, cot_seq))
    factor = 1.0 / math.sqrt(TOK_DEV * seq_count)
    layer_out = stacked[0].reshape(seq_count * TOK_DEV, D)
    input_grad = stacked[1].reshape(seq_count * TOK_DEV, D)
    return (layer_out, input_grad, totals[0] * factor, totals[1] * factor, totals[2] * factor)
```

```python
import math

import jax
import jax.numpy as jnp
from jax import lax
from jax.experimental import pallas as pl
from jax.experimental.pallas import tpu as pltpu
from jax.sharding import PartitionSpec as P

HEAD_DIM = 128
HEADS = 5
EPS = 1e-06
AXES = ("blk", "dp")
F32 = jnp.float32
BF16 = jnp.bfloat16
ORDERS = ("xyz", "yzx", "zxy")
IN_GROUPS = ((0, 1), (2, 3), (4,))
OUT_GROUPS = ((0,), (1,), (2, 3, 4))
VMEM = 56 * 1024 * 1024


def index_of(x, y, z, c):
    x, y, z = x % 4, y % 4, z % 4
    return ((y % 2) * 4 + x) * 16 + (y // 2) * 8 + z * 2 + c


def step_perm(axis, step):
    pairs = []
    for x in range(4):
        for y in range(4):
            for z in range(4):
                for c in range(2):
                    go = step if c == 0 else -step
                    to = {"x": x, "y": y, "z": z}
                    to[axis] += go
                    pairs.append((index_of(x, y, z, c), index_of(to["x"], to["y"], to["z"], c)))
    return pairs


def move(value, axis, step):
    return lax.ppermute(value, AXES, step_perm(axis, step))


def swap(value):
    return lax.ppermute(value, AXES, [(i, i ^ 1) for i in range(128)])


def block_table(groups_by_part):
    blk, dp = lax.axis_index("blk"), lax.axis_index("dp")
    core = dp % 2
    here = {"x": blk % 4, "y": (dp // 8) * 2 + blk // 4, "z": (dp // 2) % 4}
    sign = 1 - 2 * core
    out = []
    for m in range(2):
        side = sign if m == 0 else -sign
        cls = core if m == 0 else 1 - core
        for order, groups in zip(ORDERS, groups_by_part):
            n = len(groups)
            i = lax.iota(jnp.int32, 64 * n)
            k1, k2 = i % 4, (i // 4) % 4
            g, k3 = (i // 16) % n + groups[0], i // (16 * n)
            at = {a: (here[a] - side * k + 4) % 4 for a, k in zip(order, (k1, k2, k3))}
            dev = ((at["y"] % 2) * 4 + at["x"]) * 16 + (at["y"] // 2) * 8 + at["z"] * 2 + cls
            out.append(dev * 5 + g)
    return jnp.concatenate(out).astype(jnp.int32)


def call(kernel, out_shape, ins, in_specs, out_specs, scratch, flops, nbytes):
    return pl.pallas_call(
        kernel,
        out_shape=out_shape,
        in_specs=in_specs,
        out_specs=out_specs,
        scratch_shapes=scratch,
        compiler_params=pltpu.CompilerParams(vmem_limit_bytes=VMEM),
        cost_estimate=pl.CostEstimate(flops=flops, bytes_accessed=nbytes, transcendentals=0),
    )(*ins)


VM = pl.BlockSpec(memory_space=pltpu.VMEM)
SM = pl.BlockSpec(memory_space=pltpu.SMEM)
ANY = pl.BlockSpec(memory_space=pl.ANY)


def prep_kernel(tbl, x, xr, xt, rcol, rrow, work):
    total = jnp.zeros((1, 256), F32)
    rows = jnp.zeros((256, 1), F32)

    def turn(j, carry):
        total, rows = carry
        at = pl.multiple_of(j * 128, 128)
        v = x[:, pl.ds(at, 128)].astype(F32)
        rows = rows + jnp.sum(v * v, axis=1, keepdims=True)
        t = v.T
        work[pl.ds(at, 128), :] = t
        return total + jnp.sum(t * t, axis=0, keepdims=True), rows

    total, rows = lax.fori_loop(0, 40, turn, (total, rows))
    rcol[...] = lax.rsqrt(rows / 5120.0 + EPS)
    rrow[...] = lax.rsqrt(total / 5120.0 + EPS)

    def pick(i, _):
        a = work[pl.ds(pl.multiple_of(tbl[2 * i] * 8, 8), 8), :]
        b = work[pl.ds(pl.multiple_of(tbl[2 * i + 1] * 8, 8), 8), :]
        xt[pl.ds(pl.multiple_of(i * 16, 16), 16), :] = jnp.concatenate([a, b], axis=0).astype(BF16)
        return 0

    lax.fori_loop(0, 320, pick, 0, unroll=8)

    def back(j, _):
        at = pl.multiple_of(j * 128, 128)
        xr[:, pl.ds(at, 128)] = xt[pl.ds(at, 128), :].astype(F32).T.astype(BF16)
        return 0

    lax.fori_loop(0, 40, back, 0)


def prep(x, table):
    return call(
        prep_kernel,
        (
            jax.ShapeDtypeStruct((256, 5120), BF16),
            jax.ShapeDtypeStruct((5120, 256), BF16),
            jax.ShapeDtypeStruct((256, 1), F32),
            jax.ShapeDtypeStruct((1, 256), F32),
        ),
        (table, x),
        [SM, VM],
        [VM, VM, VM, VM],
        [pltpu.VMEM((5120, 256), F32)],
        10_000_000,
        8_000_000,
    )


def weight_copies(pieces, width, used, w, sems, groups_by_part):
    copies, at, n = [], 0, 0
    for m in range(2):
        for part, groups in enumerate(groups_by_part):
            for k3 in range(4):
                ref = pieces[(m * 3 + part) * 4 + k3]
                for g in range(len(groups)):
                    copies.append(
                        pltpu.make_async_copy(
                            ref.at[:, pl.ds(g * width, used)],
                            w.at[pl.ds(at, 128), :],
                            sems.at[n],
                        )
                    )
                    at += 128
                    n += 1
    return copies


def project_kernel(*refs):
    tok, rcol, pieces = refs[0], refs[1], refs[2:26]
    proj_ref, ctx_ref, wf_ref, gain_ref = refs[26:30]
    w, acc, sems = refs[30:33]
    copies = weight_copies(pieces, 1024, 1024, w, sems, IN_GROUPS)
    for c in copies:
        c.start()
    r = rcol[...]
    pickrow = (lax.broadcasted_iota(jnp.int32, (8, 128), 1) == 0).astype(BF16)
    for j in range(20):
        copies[2 * j].wait()
        copies[2 * j + 1].wait()
        rows = pl.ds(j * 256, 256)
        gcol = w[rows, pl.ds(896, 128)]
        gain_ref[rows, :] = gcol
        grow = lax.dot_general(pickrow, gcol, (((1,), (1,)), ((), ())), preferred_element_type=F32)[0:1]
        normed = (tok[:, rows].astype(F32) * r * grow).astype(BF16)
        term = jnp.dot(normed, w[rows, pl.ds(0, 896)], preferred_element_type=F32)
        if j == 0:
            acc[...] = term
        else:
            acc[...] += term
    projected = acc[...].astype(BF16)
    proj_ref[...] = projected
    attend(projected, ctx_ref, wf_ref)


def attend(projected, ctx_ref, wf_ref):
    factor = 1.0 / math.sqrt(HEAD_DIM)
    keys = projected[:, 640:768]
    values = projected[:, 768:896]
    causal = lax.broadcasted_iota(jnp.int32, (256, 256), 0) >= lax.broadcasted_iota(jnp.int32, (256, 256), 1)
    for h in range(HEADS):
        q = projected[:, h * 128 : (h + 1) * 128]
        s = lax.dot_general(q, keys, (((1,), (1,)), ((), ())), preferred_element_type=F32) * factor
        s = jnp.where(causal, s, -jnp.inf)
        e = jnp.exp(s - jnp.max(s, axis=1, keepdims=True))
        wf = e / jnp.sum(e, axis=1, keepdims=True)
        wf_ref[h] = wf
        ctx = jnp.dot(wf.astype(BF16), values, preferred_element_type=F32)
        ctx_ref[:, h * 128 : (h + 1) * 128] = ctx.astype(BF16)


def project(tok_rel, rcol, pieces):
    return call(
        project_kernel,
        (
            jax.ShapeDtypeStruct((256, 896), BF16),
            jax.ShapeDtypeStruct((256, 640), BF16),
            jax.ShapeDtypeStruct((HEADS, 256, 256), F32),
            jax.ShapeDtypeStruct((5120, 128), BF16),
        ),
        (tok_rel, rcol, *pieces),
        [VM, VM] + [ANY] * 24,
        [VM] * 4,
        [
            pltpu.VMEM((5120, 1024), BF16),
            pltpu.VMEM((256, 896), F32),
            pltpu.SemaphoreType.DMA((40,)),
        ],
        2_500_000_000,
        15_000_000,
    )


def backward_kernel(*refs):
    cot, proj, wf_ref, pieces = refs[0], refs[1], refs[2], refs[3:27]
    dproj_ref, w, acc, sems = refs[27:31]
    copies = weight_copies(pieces, 640, 640, w, sems, OUT_GROUPS)
    for c in copies:
        c.start()
    for j in range(20):
        copies[2 * j].wait()
        copies[2 * j + 1].wait()
        rows = pl.ds(j * 256, 256)
        term = jnp.dot(cot[:, rows], w[rows, :], preferred_element_type=F32)
        if j == 0:
            acc[...] = term
        else:
            acc[...] += term
    factor = 1.0 / math.sqrt(HEAD_DIM)
    keys = proj[:, 640:768]
    values = proj[:, 768:896]
    dk = jnp.zeros((256, 128), F32)
    dv = jnp.zeros((256, 128), F32)
    for h in range(HEADS):
        cols = slice(h * 128, (h + 1) * 128)
        dc = acc[:, cols].astype(BF16)
        wf = wf_ref[h]
        dw = lax.dot_general(dc, values, (((1,), (1,)), ((), ())), preferred_element_type=F32)
        ds = (wf * (dw - jnp.sum(wf * dw, axis=1, keepdims=True))).astype(BF16)
        dq = jnp.dot(ds, keys, preferred_element_type=F32) * factor
        dproj_ref[:, cols] = dq.astype(BF16)
        dk = dk + lax.dot_general(ds, proj[:, cols], (((0,), (0,)), ((), ())), preferred_element_type=F32)
        dv = dv + lax.dot_general(wf.astype(BF16), dc, (((0,), (0,)), ((), ())), preferred_element_type=F32)
    dproj_ref[:, 640:768] = (dk * factor).astype(BF16)
    dproj_ref[:, 768:896] = dv.astype(BF16)


def backward(cot_rel, projected, wf, pieces):
    return call(
        backward_kernel,
        jax.ShapeDtypeStruct((256, 896), BF16),
        (cot_rel, projected, wf, *pieces),
        [VM] * 3 + [ANY] * 24,
        VM,
        [
            pltpu.VMEM((5120, 640), BF16),
            pltpu.VMEM((256, 640), F32),
            pltpu.SemaphoreType.DMA((40,)),
        ],
        2_000_000_000,
        12_000_000,
    )


def grads_kernel(width, groups_by_part, a, a2, b, b2, *outs):
    at = 0
    for part, groups in enumerate(groups_by_part):
        for k3 in range(4):
            ref = outs[part * 4 + k3]
            for g in range(len(groups)):
                rows = pl.ds(at, 128)
                v = jnp.dot(a[rows, :], b[...], preferred_element_type=F32)
                v = v + jnp.dot(a2[rows, :], b2[...], preferred_element_type=F32)
                ref[:, g * width : (g + 1) * width] = v.astype(BF16)
                at += 128


def grads(a, a2, b, b2, groups_by_part):
    width = b.shape[1]

    def kernel(*refs):
        grads_kernel(width, groups_by_part, *refs)

    shapes = [
        jax.ShapeDtypeStruct((128, len(groups) * width), BF16)
        for groups in groups_by_part
        for _ in range(4)
    ]
    return call(
        kernel, shapes, (a, a2, b, b2), [VM] * 4, [VM] * 12, [], 2 * 2560 * 512 * width, 10_000_000
    )


def to_natural(tbl, val, nat):
    def place(i, _):
        nat[pl.ds(pl.multiple_of(tbl[i] * 8, 8), 8), :] = val[pl.ds(pl.multiple_of(i * 8, 8), 8), :]
        return 0

    lax.fori_loop(0, 640, place, 0, unroll=8)


def finish(base, nat, out):
    def turn(j, _):
        at = pl.multiple_of(j * 128, 128)
        out[:, pl.ds(at, 128)] = (base[:, pl.ds(at, 128)].astype(F32) + nat[pl.ds(at, 128), :].T).astype(BF16)
        return 0

    lax.fori_loop(0, 40, turn, 0)


def layer_kernel(*refs):
    tbl, tok, ctx, pieces = refs[0], refs[1], refs[2], refs[3:27]
    out, w, val, nat, sems = refs[27:32]
    copies = weight_copies(pieces, 640, 640, w, sems, OUT_GROUPS)
    for c in copies:
        c.start()
    for j in range(20):
        copies[2 * j].wait()
        copies[2 * j + 1].wait()
        rows = pl.ds(j * 256, 256)
        val[rows, :] = lax.dot_general(
            w[rows, :], ctx[...], (((1,), (1,)), ((), ())), preferred_element_type=F32
        )
    to_natural(tbl, val, nat)
    finish(tok, nat, out)


def layer(table, tokens, context, pieces):
    return call(
        layer_kernel,
        jax.ShapeDtypeStruct((256, 5120), BF16),
        (table, tokens, context, *pieces),
        [SM, VM, VM] + [ANY] * 24,
        VM,
        [
            pltpu.VMEM((5120, 640), BF16),
            pltpu.VMEM((5120, 256), F32),
            pltpu.VMEM((5120, 256), F32),
            pltpu.SemaphoreType.DMA((40,)),
        ],
        2_000_000_000,
        20_000_000,
    )


def input_kernel(*refs):
    tbl, cot, tokt, rrow, dproj, pieces = refs[0], refs[1], refs[2], refs[3], refs[4], refs[5:29]
    out, w, val, nat, sems = refs[29:34]
    copies = weight_copies(pieces, 1024, 1024, w, sems, IN_GROUPS)
    for c in copies:
        c.start()
    r = rrow[...]
    total = jnp.zeros((1, 256), F32)
    for j in range(20):
        copies[2 * j].wait()
        copies[2 * j + 1].wait()
        rows = pl.ds(j * 256, 256)
        dn = lax.dot_general(
            w[rows, pl.ds(0, 896)], dproj[...], (((1,), (1,)), ((), ())), preferred_element_type=F32
        )
        gain = w[rows, pl.ds(896, 128)].astype(F32)[:, 0:1]
        dn = dn * gain
        val[rows, :] = dn
        total = total + jnp.sum(tokt[rows, :].astype(F32) * r * dn, axis=0, keepdims=True)
    mean = total / 5120.0

    def settle(j, _):
        rows = pl.ds(pl.multiple_of(j * 256, 256), 256)
        val[rows, :] = r * (val[rows, :] - tokt[rows, :].astype(F32) * r * mean)
        return 0

    lax.fori_loop(0, 20, settle, 0)
    to_natural(tbl, val, nat)
    finish(cot, nat, out)


def input_side(table, cot, tokt, rrow, dproj, pieces):
    return call(
        input_kernel,
        jax.ShapeDtypeStruct((256, 5120), BF16),
        (table, cot, tokt, rrow, dproj, *pieces),
        [SM] + [VM] * 4 + [ANY] * 24,
        VM,
        [
            pltpu.VMEM((5120, 1024), BF16),
            pltpu.VMEM((5120, 256), F32),
            pltpu.VMEM((5120, 256), F32),
            pltpu.SemaphoreType.DMA((40,)),
        ],
        2_500_000_000,
        25_000_000,
    )


def spread(value, axis):
    one = move(value, axis, 1)
    three = move(value, axis, -1)
    two = move(value, axis, 2)
    return jnp.concatenate([value, one, two, three], axis=0)


def ring(value, axis):
    one = move(value, axis, 1)
    three = move(value, axis, -1)
    two = move(one, axis, 1)
    return [value, one, two, three]


def add(*values):
    total = values[0].astype(F32)
    for v in values[1:]:
        total = total + v.astype(F32)
    return total


def collect(value, axis):
    n = value.shape[0] // 4
    one = move(value[n : 2 * n], axis, -1)
    two = move(value[2 * n : 3 * n], axis, 2)
    three = move(value[3 * n :], axis, 1)
    return add(value[:n], one, two, three)


def ring_collect(parts, axis):
    far = move(parts[2], axis, -1)
    three = move(parts[3], axis, 1)
    one = move(add(parts[1], far).astype(BF16), axis, -1)
    return add(parts[0], one, three).astype(BF16)


def per_device(tokens, cotangent, in_weight, out_weight, norm_gain):
    ext = jnp.concatenate([in_weight, jnp.broadcast_to(norm_gain[:, None], (40, 128))], axis=1)
    in_pieces = [None] * 24
    out_pieces = [None] * 24
    held = []
    for order, gi, go in zip(ORDERS, IN_GROUPS, OUT_GROUPS):
        mine = jnp.concatenate(
            [ext[g * 8 : g * 8 + 8] for g in gi] + [out_weight[g * 8 : g * 8 + 8] for g in go], axis=1
        )
        held.append(spread(spread(mine, order[0]), order[1]))
    for part, (order, gi) in enumerate(zip(ORDERS, IN_GROUPS)):
        cut = len(gi) * 1024
        in_pieces[part * 4 : part * 4 + 4] = ring(held[part][:, :cut], order[2])
    for part, (order, gi) in enumerate(zip(ORDERS, IN_GROUPS)):
        cut = len(gi) * 1024
        out_pieces[part * 4 : part * 4 + 4] = ring(held[part][:, cut:], order[2])
    for i in range(12):
        in_pieces[12 + i] = swap(in_pieces[i])
    for i in range(12):
        out_pieces[12 + i] = swap(out_pieces[i])

    in_table = block_table(IN_GROUPS)
    out_table = block_table(OUT_GROUPS)
    tok_rel, tokt, rcol, rrow = prep(tokens, in_table)
    cot_rel, cott, _, _ = prep(cotangent, out_table)
    cott2 = swap(cott[2560:])

    projected, context, wf, gain_rel = project(tok_rel, rcol, in_pieces)
    normt = (tokt.astype(F32) * rrow * gain_rel[:, 0:1].astype(F32)).astype(BF16)
    normt2 = swap(normt[2560:])
    context2 = swap(context)
    out_terms = grads(cott[:2560], cott2, context, context2, OUT_GROUPS)
    dproj = backward(cot_rel, projected, wf, out_pieces)
    dproj2 = swap(dproj)
    in_terms = grads(normt[:2560], normt2, dproj, dproj2, IN_GROUPS)
    layer_out = layer(out_table, tokens, context, out_pieces)
    input_grad = input_side(in_table, cotangent, tokt, rrow, dproj, in_pieces)

    in_rows, out_rows = [], []
    sums_out = [ring_collect(out_terms[p * 4 : p * 4 + 4], ORDERS[p][2]) for p in range(3)]
    sums_in = [ring_collect(in_terms[p * 4 : p * 4 + 4], ORDERS[p][2]) for p in range(3)]
    scale = 1.0 / math.sqrt(32768.0)
    for p in range(3):
        both = jnp.concatenate([sums_in[p], sums_out[p]], axis=1)
        both = collect(both, ORDERS[p][1]).astype(BF16)
        last = collect(both, ORDERS[p][0]) * scale
        n = len(IN_GROUPS[p])
        in_rows += [last[:, g * 896 : (g + 1) * 896] for g in range(n)]
        out_rows += [
            last[:, n * 896 + g * 640 : n * 896 + (g + 1) * 640] for g in range(len(OUT_GROUPS[p]))
        ]
    in_grad = jnp.concatenate(in_rows, axis=0)
    out_grad = jnp.concatenate(out_rows, axis=0)
    gain_grad = jnp.sum(in_weight.astype(F32) * in_grad, axis=1) / norm_gain.astype(F32)
    return layer_out, input_grad, in_grad, out_grad, gain_grad


def solution(mesh):
    rows = P(AXES, None)
    return jax.shard_map(
        per_device,
        mesh=mesh,
        in_specs=(rows, rows, rows, rows, P(AXES)),
        out_specs=(rows, rows, rows, rows, P(AXES)),
        check_vma=False,
    )
```

```python
import math

import jax
import jax.numpy as jnp
from jax import lax
from jax.experimental import pallas as pl
from jax.experimental.pallas import tpu as pltpu
from jax.sharding import PartitionSpec as P

HEAD_DIM = 128
HEADS = 5
EPS = 1e-06
AXES = ("blk", "dp")
F32 = jnp.float32
BF16 = jnp.bfloat16
ORDERS = ("xyz", "yzx", "zxy")
IN_TILES = ((0, 1), (2, 3), (4,))
OUT_TILES = ((0,), (1,), (2, 3, 4))
IN_W, OUT_W = 1024, 640
VMEM = 60 * 1024 * 1024
NT = (((1,), (1,)), ((), ()))
TN = (((0,), (0,)), ((), ()))


def index_of(x, y, z, c):
    x, y, z = x % 4, y % 4, z % 4
    return ((y % 2) * 4 + x) * 16 + (y // 2) * 8 + z * 2 + c


def step_perm(axis, step):
    pairs = []
    for x in range(4):
        for y in range(4):
            for z in range(4):
                for c in range(2):
                    to = {"x": x, "y": y, "z": z}
                    to[axis] += step if c == 0 else -step
                    pairs.append((index_of(x, y, z, c), index_of(to["x"], to["y"], to["z"], c)))
    return pairs


def move(value, axis, step):
    return lax.ppermute(value, AXES, step_perm(axis, step))


def swap(value):
    return lax.ppermute(value, AXES, [(i, i ^ 1) for i in range(128)])


def chip_table(core):
    blk, dp = lax.axis_index("blk"), lax.axis_index("dp")
    here = {"x": blk % 4, "y": (dp // 8) * 2 + blk // 4, "z": (dp // 2) % 4}
    slot, u = lax.iota(jnp.int32, 64) // 8, lax.iota(jnp.int32, 64) % 8
    half = jnp.where((slot == 0) | (slot == 2) | (slot == 5) | (slot == 6), core, 1 - core)
    u = u + 8 * half
    received = (slot == 2) | (slot == 3)
    k3 = jnp.where(slot < 2, 0, jnp.where(slot >= 6, 2, jnp.where(received == (core == 0), 1, 3)))
    out = []
    for order in ORDERS:
        at = {a: (here[a] - k + 4) % 4 for a, k in zip(order, (u % 4, u // 4, k3))}
        out.append(((at["y"] % 2) * 4 + at["x"]) * 8 + (at["y"] // 2) * 4 + at["z"])
    return jnp.concatenate(out).astype(jnp.int32)


VM = pl.BlockSpec(memory_space=pltpu.VMEM)
SM = pl.BlockSpec(memory_space=pltpu.SMEM)
ANY = pl.BlockSpec(memory_space=pl.ANY)


def call(kernel, out_shape, ins, in_specs, out_specs, scratch, flops, nbytes):
    return pl.pallas_call(
        kernel,
        out_shape=out_shape,
        in_specs=in_specs,
        out_specs=out_specs,
        scratch_shapes=scratch,
        compiler_params=pltpu.CompilerParams(vmem_limit_bytes=VMEM),
        cost_estimate=pl.CostEstimate(flops=flops, bytes_accessed=nbytes, transcendentals=0),
    )(*ins)


def gain_row(block):
    first = (lax.broadcasted_iota(jnp.int32, (8, 128), 1) == 0).astype(BF16)
    return lax.dot_general(first, block, NT, preferred_element_type=F32)[0:1]


SLOTS = tuple((i * 128, 128) for i in range(8))


def core_kernel(*refs):
    tbl, tok, rcol, cot = refs[:4]
    pieces = refs[4:28]
    ctx_ref, dproj_ref, gain_ref, win, wout = refs[28:33]
    held = refs[33:36]
    acc, dacc, sems = refs[36:39]
    copies = []
    for p in range(3):
        for i, (at, n) in enumerate(SLOTS):
            copies.append(
                pltpu.make_async_copy(pieces[p * 8 + i], held[p].at[pl.ds(at, n), :], sems.at[p * 8 + i])
            )
    for c in copies:
        c.start()
    for p in range(3):
        ni = len(IN_TILES[p])
        for i, (at, n) in enumerate(SLOTS):
            copies[p * 8 + i].wait()

            def place(s, _, p=p, ni=ni):
                src = pl.ds(pl.multiple_of(s * 16, 16), 16)
                base = tbl[p * 64 + s] * 80
                for g, t in enumerate(IN_TILES[p]):
                    win[pl.ds(pl.multiple_of(base + t * 16, 16), 16), :] = held[p][
                        src, g * IN_W : (g + 1) * IN_W
                    ]
                for g, t in enumerate(OUT_TILES[p]):
                    lanes = slice(ni * IN_W + g * OUT_W, ni * IN_W + (g + 1) * OUT_W)
                    wout[pl.ds(pl.multiple_of(base + t * 16, 16), 16), :] = held[p][src, lanes]
                return 0

            lax.fori_loop(at // 16, (at + n) // 16, place, 0, unroll=4)
    to = 0
    for p in range(3):
        for first, count in ROLES:
            for g in range(len(IN_TILES[p])):
                lanes = slice(g * IN_W + 896, (g + 1) * IN_W)
                gain_ref[to : to + count * 16, :] = held[p][first * 16 : (first + count) * 16, lanes]
                to += count * 16
    r = rcol[...]
    for j in range(10):
        rows = pl.ds(j * 512, 512)
        gcol = win[rows, 896:1024]
        normed = (tok[:, rows].astype(F32) * r * gain_row(gcol)).astype(BF16)
        term = jnp.dot(normed, win[rows, 0:896], preferred_element_type=F32)
        dterm = jnp.dot(cot[:, rows], wout[rows, :], preferred_element_type=F32)
        if j == 0:
            acc[...] = term
            dacc[...] = dterm
        else:
            acc[...] += term
            dacc[...] += dterm
    factor = 1.0 / math.sqrt(HEAD_DIM)
    keys = acc[:, 640:768].astype(BF16)
    values = acc[:, 768:896].astype(BF16)
    causal = lax.broadcasted_iota(jnp.int32, (256, 256), 0) >= lax.broadcasted_iota(jnp.int32, (256, 256), 1)
    dk = jnp.zeros((256, 128), F32)
    dv = jnp.zeros((256, 128), F32)
    for h in range(HEADS):
        cols = slice(h * 128, (h + 1) * 128)
        q = acc[:, cols].astype(BF16)
        dc = dacc[:, cols].astype(BF16)
        s = lax.dot_general(q, keys, NT, preferred_element_type=F32) * factor
        s = jnp.where(causal, s, -jnp.inf)
        e = jnp.exp(s - jnp.max(s, axis=1, keepdims=True))
        wf = e / jnp.sum(e, axis=1, keepdims=True)
        wb = wf.astype(BF16)
        ctx_ref[:, cols] = jnp.dot(wb, values, preferred_element_type=F32).astype(BF16)
        dw = lax.dot_general(dc, values, NT, preferred_element_type=F32)
        ds = (wf * (dw - jnp.sum(wf * dw, axis=1, keepdims=True))).astype(BF16)
        dq = jnp.dot(ds, keys, preferred_element_type=F32) * factor
        dproj_ref[:, cols] = dq.astype(BF16)
        dk = dk + lax.dot_general(ds, q, TN, preferred_element_type=F32)
        dv = dv + lax.dot_general(wb, dc, TN, preferred_element_type=F32)
    dproj_ref[:, 640:768] = (dk * factor).astype(BF16)
    dproj_ref[:, 768:896] = dv.astype(BF16)


def widths(in_w):
    return [len(a) * in_w + len(b) * OUT_W for a, b in zip(IN_TILES, OUT_TILES)]


def core_call(table, tokens, rcol, cotangent, pieces):
    return call(
        core_kernel,
        (
            jax.ShapeDtypeStruct((256, 640), BF16),
            jax.ShapeDtypeStruct((256, 896), BF16),
            jax.ShapeDtypeStruct((3200, 128), BF16),
            jax.ShapeDtypeStruct((5120, IN_W), BF16),
            jax.ShapeDtypeStruct((5120, OUT_W), BF16),
        ),
        (table, tokens, rcol, cotangent, *pieces),
        [SM, VM, VM, VM] + [ANY] * 24,
        [VM] * 5,
        [pltpu.VMEM((1024, w), BF16) for w in widths(IN_W)]
        + [
            pltpu.VMEM((256, 896), F32),
            pltpu.VMEM((256, 640), F32),
            pltpu.SemaphoreType.DMA((24,)),
        ],
        4_500_000_000,
        40_000_000,
    )


ROLES = ((48, 8), (16, 8), (24, 8), (0, 16))


def arrange_kernel(tbl, tbl2, tt, ct, in_own, out_own, in_other, out_other):
    def fill(table, out, source, tiles):
        at = 0
        for p in range(3):
            for first, count in ROLES:
                for t in tiles[p]:

                    def unit(u, _, p=p, t=t, first=first, at=at):
                        src = pl.ds(pl.multiple_of(table[p * 64 + first + u] * 80 + t * 16, 16), 16)
                        out[pl.ds(pl.multiple_of(at + u * 16, 16), 16), :] = source[src, :]
                        return 0

                    lax.fori_loop(0, count, unit, 0, unroll=8)
                    at += count * 16

    fill(tbl, in_own, tt, IN_TILES)
    fill(tbl, out_own, ct, OUT_TILES)
    fill(tbl2, in_other, tt, IN_TILES)
    fill(tbl2, out_other, ct, OUT_TILES)


def arrange(table, other, tt, ct):
    return call(
        arrange_kernel,
        (jax.ShapeDtypeStruct((3200, 256), BF16),) * 4,
        (table, other, tt, ct),
        [SM] * 2 + [VM] * 2,
        [VM] * 4,
        [],
        1_000_000,
        12_000_000,
    )


def grads_kernel(in_own, in_other, out_own, out_other, rr, rr2, gain, dp, dp2, cx, cx2, *rest):
    outs, held, dpb, cxb, sems = rest[:12], rest[12:24], rest[24], rest[25], rest[26]
    dpb[0:256, :] = dp[...]
    dpb[256:512, :] = dp2[...]
    cxb[0:256, :] = cx[...]
    cxb[256:512, :] = cx2[...]
    starts = []
    in_at, out_at = 0, 0
    for p in range(3):
        for role, (_, count) in enumerate(ROLES):
            starts.append((p, role, count * 16, in_at, out_at))
            in_at += count * 16 * len(IN_TILES[p])
            out_at += count * 16 * len(OUT_TILES[p])
    starts.sort(key=lambda v: v[1])
    copies = []
    for p, role, n, i, o in starts:
        ni = len(IN_TILES[p])
        out = held[p * 4 + role]
        for g in range(ni):
            gc = gain[i : i + n, :].astype(F32)[:, 0:1]
            lhs = (in_own[i : i + n, :].astype(F32) * rr[...] * gc).astype(BF16)
            lhs2 = (in_other[i : i + n, :].astype(F32) * rr2[...] * gc).astype(BF16)
            v = jnp.dot(jnp.concatenate([lhs, lhs2], axis=1), dpb[...], preferred_element_type=F32)
            out[:, g * 896 : (g + 1) * 896] = v.astype(BF16)
            i += n
        for g in range(len(OUT_TILES[p])):
            lhs = jnp.concatenate([out_own[o : o + n, :], out_other[o : o + n, :]], axis=1)
            v = jnp.dot(lhs, cxb[...], preferred_element_type=F32)
            to = ni * 896 + g * OUT_W
            out[:, to : to + OUT_W] = v.astype(BF16)
            o += n
        c = pltpu.make_async_copy(out, outs[p * 4 + role], sems.at[p * 4 + role])
        c.start()
        copies.append(c)
    for c in copies:
        c.wait()


def grads(operands):
    sizes = [(count * 16, w) for w in widths(896) for _, count in ROLES]
    return call(
        grads_kernel,
        [jax.ShapeDtypeStruct(v, BF16) for v in sizes],
        operands,
        [VM] * 11,
        [ANY] * 12,
        [pltpu.VMEM(v, BF16) for v in sizes]
        + [
            pltpu.VMEM((512, 896), BF16),
            pltpu.VMEM((512, OUT_W), BF16),
            pltpu.SemaphoreType.DMA((12,)),
        ],
        5_000_000_000,
        20_000_000,
    )


def stepped(kernel, out_shape, ins, in_specs, out_specs, scratch, steps, flops, nbytes):
    return pl.pallas_call(
        kernel,
        out_shape=out_shape,
        grid=(steps,),
        in_specs=in_specs,
        out_specs=out_specs,
        scratch_shapes=scratch,
        compiler_params=pltpu.CompilerParams(vmem_limit_bytes=VMEM),
        cost_estimate=pl.CostEstimate(flops=flops, bytes_accessed=nbytes, transcendentals=0),
    )(*ins)


def layer_kernel(tok, ctx, wout, out):
    v = lax.dot_general(ctx[...], wout[...], NT, preferred_element_type=F32)
    out[...] = (tok[...].astype(F32) + v).astype(BF16)


def layer(tokens, context, wout):
    return stepped(
        layer_kernel,
        jax.ShapeDtypeStruct((256, 5120), BF16),
        (tokens, context, wout),
        [
            pl.BlockSpec((256, 1024), lambda j: (0, j)),
            pl.BlockSpec((256, OUT_W), lambda j: (0, 0)),
            pl.BlockSpec((1024, OUT_W), lambda j: (j, 0)),
        ],
        pl.BlockSpec((256, 1024), lambda j: (0, j)),
        [],
        5,
        2_000_000_000,
        12_000_000,
    )


def input_kernel(cot, tok, rcol, dproj, win, out, val, scaled, total):
    j = pl.program_id(0)
    cols = pl.ds(pl.multiple_of(j * 512, 512), 512)
    r = rcol[...]
    dn = lax.dot_general(dproj[...], win[:, 0:896], NT, preferred_element_type=F32)
    dn = dn * gain_row(win[:, 896:1024])
    sc = tok[...].astype(F32) * r
    val[:, cols] = dn
    scaled[:, cols] = sc
    part = jnp.sum(sc * dn, axis=1, keepdims=True)

    @pl.when(j == 0)
    def _():
        total[...] = part

    @pl.when(j > 0)
    def _():
        total[...] += part

    @pl.when(j == 9)
    def _():
        mean = total[...] / 5120.0
        for i in range(10):
            at = slice(i * 512, (i + 1) * 512)
            v = r * (val[:, at] - scaled[:, at] * mean)
            out[:, at] = (cot[:, at].astype(F32) + v).astype(BF16)


def input_side(cot, tok, rcol, dproj, win):
    whole = lambda shape: pl.BlockSpec(shape, lambda j: (0, 0))
    return stepped(
        input_kernel,
        jax.ShapeDtypeStruct((256, 5120), BF16),
        (cot, tok, rcol, dproj, win),
        [
            whole((256, 5120)),
            pl.BlockSpec((256, 512), lambda j: (0, j)),
            whole((256, 1)),
            whole((256, 896)),
            pl.BlockSpec((512, IN_W), lambda j: (j, 0)),
        ],
        whole((256, 5120)),
        [pltpu.VMEM((256, 5120), F32), pltpu.VMEM((256, 5120), F32), pltpu.VMEM((256, 1), F32)],
        10,
        2_500_000_000,
        18_000_000,
    )


def first_join(corev, held, r1, q1, r2):
    def kernel(c, *refs):
        core = c[0]
        for p in range(3):
            x, one, other, two = refs[p * 4 : p * 4 + 4]
            out, half = refs[12 + p], refs[15 + p]
            out[0:16, :] = x[...]
            out[pl.ds(pl.multiple_of(16 + 32 * core, 16), 16), :] = one[...]
            out[32:48, :] = two[...]
            out[pl.ds(pl.multiple_of(48 - 32 * core, 16), 16), :] = other[...]
            half[...] = out[pl.ds(pl.multiple_of(32 * core, 16), 32), :]

    ins = [v for p in range(3) for v in (held[p], r1[p], q1[p], r2[p])]
    shapes = [jax.ShapeDtypeStruct((n, w), BF16) for n in (64, 32) for w in widths(IN_W)]
    out = call(kernel, shapes, (corev, *ins), [SM] + [VM] * 12, [VM] * 6, [], 1_000, 4_000_000)
    return out[:3], out[3:]


def second_join(corev, held, r1, q1, r2, q2):
    def kernel(c, *refs):
        core = c[0]
        sems, outs = refs[24], []
        ins = []
        for p in range(3):
            whole = refs[21 + p]
            at = (0, 64 + 128 * core, 192 - 128 * core, 128 + 32 * core, 160 - 32 * core)
            for i in range(5):
                ref = refs[p * 5 + i]
                to = whole.at[pl.ds(pl.multiple_of(at[i], 16), ref.shape[0]), :]
                ins.append(pltpu.make_async_copy(ref, to, sems.at[p * 7 + i]))
        for m in ins:
            m.start()
        for p in range(3):
            for m in ins[p * 5 : p * 5 + 5]:
                m.wait()
            for i in range(2):
                at = 128 * core if i == 0 else 128 - 128 * core
                src = refs[21 + p].at[pl.ds(pl.multiple_of(at, 16), 128), :]
                m = pltpu.make_async_copy(src, refs[15 + i * 3 + p], sems.at[p * 7 + 5 + i])
                m.start()
                outs.append(m)
        for m in outs:
            m.wait()

    ins = [v for p in range(3) for v in (held[p], r1[p], q1[p], r2[p], q2[p])]
    shapes = [jax.ShapeDtypeStruct((128, w), BF16) for _ in range(2) for w in widths(IN_W)]
    scratch = [pltpu.VMEM((256, w), BF16) for w in widths(IN_W)] + [pltpu.SemaphoreType.DMA((21,))]
    out = call(kernel, shapes, (corev, *ins), [SM] + [ANY] * 15, [ANY] * 6, scratch, 1_000, 9_000_000)
    return out[:3], out[3:]


def first_sum(corev, own, ra, rb, qa, qb):
    rows = (192, 128, 64, 64, 128)

    def kernel(c, *refs):
        core = c[0]
        work, sems = refs[24:27], refs[42]
        ins, outs = [], []
        for p in range(3):
            for i in range(5):
                src = refs[p * 5 + i].at[pl.ds(0, rows[i]), :]
                ins.append(pltpu.make_async_copy(src, refs[27 + p * 5 + i], sems.at[p * 5 + i]))
        for m in ins:
            m.start()
        for p in range(3):
            for m in ins[p * 5 : p * 5 + 5]:
                m.wait()
            o, a, b, xa, xb = refs[27 + p * 5 : 32 + p * 5]
            w = work[p]
            f = lambda ref, at: ref[at : at + 64, :].astype(F32)
            w[0:64, :] = (f(o, 0) + f(a, 0) + f(xb, 0)).astype(BF16)
            w[64:128, :] = (f(o, 128) + f(b, 0) + f(xa, 0)).astype(BF16)
            w[128:192, :] = (f(o, 64) + f(a, 64) + f(xb, 64)).astype(BF16)
            for i, (at, n) in enumerate(((64 * core, 64), (128, 64), (64 - 32 * core, 32))):
                src = w.at[pl.ds(pl.multiple_of(at, 16), n), :]
                m = pltpu.make_async_copy(src, refs[15 + i * 3 + p], sems.at[15 + p * 3 + i])
                m.start()
                outs.append(m)
        for m in outs:
            m.wait()

    ins = [v for p in range(3) for v in (own[p], ra[p], rb[p], qa[p], qb[p])]
    shapes = [jax.ShapeDtypeStruct((n, w), BF16) for n in (64, 64, 32) for w in widths(896)]
    scratch = [pltpu.VMEM((192, w), BF16) for w in widths(896)]
    scratch += [pltpu.VMEM((n, w), BF16) for w in widths(896) for n in rows]
    scratch += [pltpu.SemaphoreType.DMA((24,))]
    out = call(kernel, shapes, (corev, *ins), [SM] + [ANY] * 15, [ANY] * 9, scratch, 1_000, 12_000_000)
    return out[:3], out[3:6], out[6:]


def second_sum(corev, zero, r1, q1, r2, q2):
    def kernel(c, *refs):
        core = c[0]
        for p in range(3):
            z, a, b, e, g = refs[p * 5 : p * 5 + 5]
            own, one, two, work = refs[15 + p], refs[18 + p], refs[21 + p], refs[24 + p]
            f = lambda ref: ref[...].astype(F32)
            work[...] = f(z) + f(a) + f(b)
            work[pl.ds(pl.multiple_of(32 * core, 16), 32), :] += f(e)
            work[pl.ds(pl.multiple_of(32 - 32 * core, 16), 32), :] += f(g)
            own[...] = work[0:16, :].astype(BF16)
            one[...] = work[pl.ds(pl.multiple_of(16 + 32 * core, 16), 16), :].astype(BF16)
            two[...] = work[32:48, :].astype(BF16)

    ins = [v for p in range(3) for v in (zero[p], r1[p], q1[p], r2[p], q2[p])]
    shapes = [jax.ShapeDtypeStruct((16, w), BF16) for _ in range(3) for w in widths(896)]
    scratch = [pltpu.VMEM((64, w), F32) for w in widths(896)]
    out = call(kernel, shapes, (corev, *ins), [SM] + [VM] * 15, [VM] * 9, scratch, 1_000, 4_000_000)
    return out[:3], out[3:6], out[6:]


def each(function, *lists):
    return [function(p, *(v[p] for v in lists)) for p in range(3)]


def along(stage, step):
    return lambda p, value: move(value, ORDERS[p][stage], step)


def swapped(values):
    return [swap(v) for v in values]


def per_device(tokens, cotangent, in_weight, out_weight, norm_gain):
    core = lax.axis_index("dp") % 2
    first = core == 0
    mine = jnp.concatenate(
        [in_weight, jnp.broadcast_to(norm_gain[:, None], (40, 128)), out_weight], axis=1
    )
    other = swap(mine)
    chip = jnp.concatenate([jnp.where(first, mine, other), jnp.where(first, other, mine)], axis=0)
    held = []
    for ti, to in zip(IN_TILES, OUT_TILES):
        held.append(
            jnp.concatenate(
                [chip[t * 16 : t * 16 + 16, :IN_W] for t in ti]
                + [chip[t * 16 : t * 16 + 16, IN_W:] for t in to],
                axis=1,
            )
        )
    corev = core.astype(jnp.int32).reshape(1)
    table, other_table = chip_table(core), chip_table(1 - core)
    tie = lax.optimization_barrier
    r1 = each(along(0, 1), held)
    r2 = each(along(0, 2), held)
    cott = cotangent.T
    r2, cott = tie((r2, cott))
    held, half = first_join(corev, held, r1, swapped(r1), r2)
    late_tokens, _ = tie((tokens, held))
    x = late_tokens.astype(F32)
    rcol = lax.rsqrt(jnp.mean(x * x, axis=1, keepdims=True) + EPS)
    tokt = late_tokens.T
    r1 = each(along(1, 1), held)
    r2 = each(along(1, 2), half)
    r2, tokt, rcol = tie((r2, tokt, rcol))
    rrow = rcol.reshape(1, 256)
    own_a, own_b = second_join(corev, held, r1, swapped(r1), r2, swapped(r2))
    got_a = each(along(2, 1), own_a)
    got_b = each(along(2, 1), own_b)
    far = each(along(2, 1), got_a)
    tokt, cott, _ = tie((tokt, cott, own_a))
    in_own, out_own, in_other, out_other = arrange(table, other_table, tokt, cott)
    got_b[2], in_own, out_own, in_other, out_other = tie((got_b[2], in_own, out_own, in_other, out_other))
    swap_a = [tie((got_a[p], got_b[p]))[0] for p in range(3)]
    slots = [own_a, own_b, got_a, got_b, swapped(swap_a), swapped(got_b), far, swapped(far)]
    pieces = [slot[p] for p in range(3) for slot in slots]
    in_other, out_other, rrow2, _ = tie((in_other, out_other, rrow, far))
    in_other, out_other, rrow2 = swap(in_other), swap(out_other), swap(rrow2)

    context, dproj, gain, win, wout = core_call(table, tokens, rcol, cotangent, pieces)
    context2, dproj2 = swap(context), swap(dproj)
    terms = grads(
        (in_own, in_other, out_own, out_other, rrow, rrow2, gain, dproj, dproj2, context, context2)
    )
    far, near_a, near_b, own = terms[0::4], terms[1::4], terms[2::4], terms[3::4]
    got = each(along(2, -1), far)
    rb = each(along(2, -1), near_b)
    near_a = [(near_a[p].astype(F32) + got[p].astype(F32)).astype(BF16) for p in range(3)]
    ra = each(along(2, -1), near_a)
    late_tokens, late_cot, _ = tie((tokens, cotangent, near_a))
    layer_out = layer(late_tokens, context, wout)
    rb, layer_out = tie((rb, layer_out))
    input_grad = input_side(late_cot, tokens, rcol, dproj, win)
    ra, input_grad = tie((ra, input_grad))

    zero, one, two = first_sum(corev, own, ra, rb, swapped(ra), swapped(rb))
    r1 = each(along(1, -1), one)
    r2 = each(along(1, 2), two)
    zero, one, two = second_sum(corev, zero, r1, swapped(r1), r2, swapped(r2))
    r1 = each(along(0, -1), one)
    r2 = each(along(0, 2), two)
    q1 = swapped(r1)
    f = lambda v: v.astype(F32)
    sums = [f(zero[p]) + f(r1[p]) + f(q1[p]) + f(r2[p]) for p in range(3)]
    scale = 1.0 / math.sqrt(32768.0)
    in_rows, out_rows = [], []
    for p in range(3):
        n = len(IN_TILES[p])
        in_rows += [sums[p][:, g * 896 : (g + 1) * 896] for g in range(n)]
        out_rows += [
            sums[p][:, n * 896 + g * OUT_W : n * 896 + (g + 1) * OUT_W] for g in range(len(OUT_TILES[p]))
        ]
    in_grad = lax.dynamic_slice_in_dim(jnp.concatenate(in_rows, axis=0), core * 40, 40, 0) * scale
    out_grad = lax.dynamic_slice_in_dim(jnp.concatenate(out_rows, axis=0), core * 40, 40, 0) * scale
    gain_grad = jnp.sum(in_weight.astype(F32) * in_grad, axis=1) / norm_gain.astype(F32)
    return layer_out, input_grad, in_grad, out_grad, gain_grad


def solution(mesh):
    rows = P(AXES, None)
    return jax.shard_map(
        per_device,
        mesh=mesh,
        in_specs=(rows, rows, rows, rows, P(AXES)),
        out_specs=(rows, rows, rows, rows, P(AXES)),
        check_vma=False,
    )
```

```python
import math

import jax
import jax.numpy as jnp
from jax import lax
from jax.experimental import pallas as pl
from jax.experimental.pallas import tpu as pltpu
from jax.sharding import PartitionSpec as P

HEAD_DIM = 128
HEADS = 5
EPS = 1e-06
AXES = ("blk", "dp")
F32 = jnp.float32
BF16 = jnp.bfloat16
ORDERS = ("xyz", "yzx", "zxy")
IN_TILES = ((0, 1), (2, 3), (4,))
OUT_TILES = ((0,), (1,), (2, 3, 4))
IN_W, OUT_W = 1024, 640
MIB = 1024 * 1024
NT = (((1,), (1,)), ((), ()))
TN = (((0,), (0,)), ((), ()))


def index_of(x, y, z, c):
    x, y, z = x % 4, y % 4, z % 4
    return ((y % 2) * 4 + x) * 16 + (y // 2) * 8 + z * 2 + c


def step_perm(axis, step):
    pairs = []
    for x in range(4):
        for y in range(4):
            for z in range(4):
                for c in range(2):
                    to = {"x": x, "y": y, "z": z}
                    to[axis] += step if c == 0 else -step
                    pairs.append((index_of(x, y, z, c), index_of(to["x"], to["y"], to["z"], c)))
    return pairs


def move(value, axis, step):
    return lax.ppermute(value, AXES, step_perm(axis, step))


def swap(value):
    return lax.ppermute(value, AXES, [(i, i ^ 1) for i in range(128)])


def chip_table(core):
    blk, dp = lax.axis_index("blk"), lax.axis_index("dp")
    here = {"x": blk % 4, "y": (dp // 8) * 2 + blk // 4, "z": (dp // 2) % 4}
    slot, u = lax.iota(jnp.int32, 64) // 8, lax.iota(jnp.int32, 64) % 8
    half = jnp.where((slot == 0) | (slot == 2) | (slot == 5) | (slot == 6), core, 1 - core)
    u = u + 8 * half
    received = (slot == 2) | (slot == 3)
    k3 = jnp.where(slot < 2, 0, jnp.where(slot >= 6, 2, jnp.where(received == (core == 0), 1, 3)))
    out = []
    for order in ORDERS:
        at = {a: (here[a] - k + 4) % 4 for a, k in zip(order, (u % 4, u // 4, k3))}
        out.append(((at["y"] % 2) * 4 + at["x"]) * 8 + (at["y"] // 2) * 4 + at["z"])
    return jnp.concatenate(out).astype(jnp.int32)


VM = pl.BlockSpec(memory_space=pltpu.VMEM)
SM = pl.BlockSpec(memory_space=pltpu.SMEM)
ANY = pl.BlockSpec(memory_space=pl.ANY)


def call(kernel, out_shape, ins, in_specs, out_specs, scratch, flops, nbytes, mib):
    return pl.pallas_call(
        kernel,
        out_shape=out_shape,
        in_specs=in_specs,
        out_specs=out_specs,
        scratch_shapes=scratch,
        compiler_params=pltpu.CompilerParams(vmem_limit_bytes=mib * MIB),
        cost_estimate=pl.CostEstimate(flops=flops, bytes_accessed=nbytes, transcendentals=0),
    )(*ins)


def gain_row(block):
    first = (lax.broadcasted_iota(jnp.int32, (8, 128), 1) == 0).astype(BF16)
    return lax.dot_general(first, block, NT, preferred_element_type=F32)[0:1]


def core_kernel(*refs):
    tbl, rcol, tok_in, cot_in = refs[:4]
    pieces = refs[4:28]
    ctx_ref, dproj_ref, gain_ref, win_out, wout_out = refs[28:33]
    held, (win, wout, tok, cot, acc, dacc, sems) = refs[33:36], refs[36:43]
    loads = [
        pltpu.make_async_copy(
            pieces[p * 8 + i], held[p].at[pl.ds(i * 128, 128), :], sems.at[p * 8 + i]
        )
        for p in range(3)
        for i in range(8)
    ]
    for c in loads:
        c.start()
    acts = [
        pltpu.make_async_copy(tok_in, tok, sems.at[24]),
        pltpu.make_async_copy(cot_in, cot, sems.at[25]),
    ]
    for c in acts:
        c.start()
    copies = []
    for p in range(3):
        ni = len(IN_TILES[p])
        for slot in range(8):
            loads[p * 8 + slot].wait()

            def place(u, _, p=p, ni=ni, slot=slot):
                src = pl.ds(pl.multiple_of(slot * 128 + u * 16, 16), 16)
                chip = tbl[p * 64 + slot * 8 + u]
                for g, t in enumerate(IN_TILES[p]):
                    win[chip, t * 16 : t * 16 + 16, :] = held[p][src, g * IN_W : (g + 1) * IN_W]
                for g, t in enumerate(OUT_TILES[p]):
                    at = ni * IN_W + g * OUT_W
                    wout[chip, t * 16 : t * 16 + 16, :] = held[p][src, at : at + OUT_W]
                return 0

            lax.fori_loop(0, 8, place, 0, unroll=4)
    for w, out in ((win, win_out), (wout, wout_out)):
        for i in range(2):
            chips = pl.ds(i * 32, 32)
            n = 26 + len(copies)
            copies.append(pltpu.make_async_copy(w.at[chips], out.at[chips], sems.at[n]))
            copies[-1].start()
    to = 0
    for first, count in ROLES:
        for p in range(3):
            for g in range(len(IN_TILES[p])):
                lanes = slice(g * IN_W + 896, (g + 1) * IN_W)
                gain_ref[to : to + count * 16, :] = held[p][first * 16 : (first + count) * 16, lanes]
                to += count * 16
    for c in acts:
        c.wait()
    r = rcol[...]
    for j in range(4):
        rows = pl.ds(j * 1280, 1280)
        chips = slice(j * 16, (j + 1) * 16)
        wi = win[chips].reshape(1280, IN_W)
        normed = (tok[:, rows].astype(F32) * r * gain_row(wi[:, 896:1024])).astype(BF16)
        term = jnp.dot(normed, wi[:, 0:896], preferred_element_type=F32)
        wo = wout[chips].reshape(1280, OUT_W)
        dterm = jnp.dot(cot[:, rows], wo, preferred_element_type=F32)
        if j == 0:
            acc[...] = term
            dacc[...] = dterm
        else:
            acc[...] += term
            dacc[...] += dterm
    factor = 1.0 / math.sqrt(HEAD_DIM)
    keys = acc[:, 640:768].astype(BF16)
    values = acc[:, 768:896].astype(BF16)
    causal = lax.broadcasted_iota(jnp.int32, (256, 256), 0) >= lax.broadcasted_iota(jnp.int32, (256, 256), 1)
    dk = jnp.zeros((256, 128), F32)
    dv = jnp.zeros((256, 128), F32)
    for h in range(HEADS):
        cols = slice(h * 128, (h + 1) * 128)
        q = acc[:, cols].astype(BF16)
        dc = dacc[:, cols].astype(BF16)
        s = lax.dot_general(q, keys, NT, preferred_element_type=F32) * factor
        s = jnp.where(causal, s, -jnp.inf)
        e = jnp.exp(s - jnp.max(s, axis=1, keepdims=True))
        wf = e / jnp.sum(e, axis=1, keepdims=True)
        wb = wf.astype(BF16)
        ctx_ref[:, cols] = jnp.dot(wb, values, preferred_element_type=F32).astype(BF16)
        dw = lax.dot_general(dc, values, NT, preferred_element_type=F32)
        ds = (wf * (dw - jnp.sum(wf * dw, axis=1, keepdims=True))).astype(BF16)
        dq = jnp.dot(ds, keys, preferred_element_type=F32) * factor
        dproj_ref[:, cols] = dq.astype(BF16)
        dk = dk + lax.dot_general(ds, q, TN, preferred_element_type=F32)
        dv = dv + lax.dot_general(wb, dc, TN, preferred_element_type=F32)
    dproj_ref[:, 640:768] = (dk * factor).astype(BF16)
    dproj_ref[:, 768:896] = dv.astype(BF16)
    for c in copies:
        c.wait()


def widths(in_w):
    return [len(a) * in_w + len(b) * OUT_W for a, b in zip(IN_TILES, OUT_TILES)]


def core_call(table, tokens, rcol, cotangent, pieces):
    return call(
        core_kernel,
        (
            jax.ShapeDtypeStruct((256, 640), BF16),
            jax.ShapeDtypeStruct((256, 896), BF16),
            jax.ShapeDtypeStruct((3200, 128), BF16),
            jax.ShapeDtypeStruct((64, 80, IN_W), BF16),
            jax.ShapeDtypeStruct((64, 80, OUT_W), BF16),
        ),
        (table, rcol, tokens, cotangent, *pieces),
        [SM, VM] + [ANY] * 26,
        [VM] * 3 + [ANY] * 2,
        [pltpu.VMEM((1024, w), BF16) for w in widths(IN_W)]
        + [
            pltpu.VMEM((64, 80, IN_W), BF16),
            pltpu.VMEM((64, 80, OUT_W), BF16),
            pltpu.VMEM((256, 5120), BF16),
            pltpu.VMEM((256, 5120), BF16),
            pltpu.VMEM((256, 896), F32),
            pltpu.VMEM((256, 640), F32),
            pltpu.SemaphoreType.DMA((32,)),
        ],
        4_500_000_000,
        40_000_000,
        60,
    )


ROLES = ((48, 8), (24, 8), (16, 8), (0, 16))


def arrange_kernel(tbl, tbl2, tok, cot, own, other, tt, ct):
    def turn(j, _):
        at = pl.multiple_of(j * 128, 128)
        tt[pl.ds(at, 128), :] = tok[:, pl.ds(at, 128)].T
        ct[pl.ds(at, 128), :] = cot[:, pl.ds(at, 128)].T
        return 0

    lax.fori_loop(0, 40, turn, 0, unroll=2)
    for table, out in ((tbl, own), (tbl2, other)):
        at = 0
        for first, count in ROLES:
            for source, tiles in ((tt, IN_TILES), (ct, OUT_TILES)):
                for p in range(3):
                    for t in tiles[p]:

                        def unit(u, _, p=p, t=t, first=first, at=at, table=table, out=out, source=source):
                            row = table[p * 64 + first + u] * 80 + t * 16
                            src = pl.ds(pl.multiple_of(row, 16), 16)
                            out[pl.ds(pl.multiple_of(at + u * 16, 16), 16), :] = source[src, :]
                            return 0

                        lax.fori_loop(0, count, unit, 0, unroll=8)
                        at += count * 16


def arrange(table, other, tokens, cotangent):
    return call(
        arrange_kernel,
        (jax.ShapeDtypeStruct((6400, 256), BF16),) * 2,
        (table, other, tokens, cotangent),
        [SM] * 2 + [VM] * 2,
        [VM] * 2,
        [pltpu.VMEM((5120, 256), BF16)] * 2,
        1_000_000,
        12_000_000,
        22,
    )


def grads(role, rows, operands, extra=(), roles=1):
    count = ROLES[role][1] * 16
    first = sum(c * 16 * 5 for _, c in ROLES[:role])
    total = count * 5 * roles
    n_extra = len(extra[0]) if extra else 0
    plan = [(v.shape[0], at) for v, at in extra[0]] if extra else []

    def kernel(*refs):
        sources, (rr, rr2, dp, dp2, cx, cx2) = refs[:3], refs[3:9]
        adds = refs[9 : 9 + 3 * n_extra]
        outs = refs[9 + 3 * n_extra : 9 + 3 * (n_extra + roles)]
        mine, theirs, gain, dpb, cxb, sems = refs[9 + 3 * (n_extra + roles) :]
        loads = [
            pltpu.make_async_copy(src.at[pl.ds(first * n, total * n), :], to, sems.at[i])
            for i, (src, to, n) in enumerate(zip(sources, (mine, theirs, gain), (2, 2, 1)))
        ]
        for c in loads:
            c.start()
        dpb[0:256, :] = dp[...]
        dpb[256:512, :] = dp2[...]
        cxb[0:256, :] = cx[...]
        cxb[256:512, :] = cx2[...]
        for c in loads:
            c.wait()
        used = 0
        for q in range(3 * roles):
            p = q % 3
            if p == 0:
                i = q // 3 * count * 10
                o = i + count * 5
            ni = len(IN_TILES[p])

            def put(v, lanes, p=p, q=q):
                for k, (n, at) in enumerate(plan):
                    more = adds[p * n_extra + k][:, lanes].astype(F32)
                    parts = [v[:at]] if at else []
                    parts.append(v[at : at + n] + more)
                    if at + n < rows:
                        parts.append(v[at + n :])
                    v = parts[0] if len(parts) == 1 else jnp.concatenate(parts, axis=0)
                outs[q][:, lanes] = v.astype(BF16)

            for g in range(ni):
                gc = gain[used : used + rows, :].astype(F32)[:, 0:1]
                used += count
                lhs = (mine[i : i + rows, :].astype(F32) * rr[...] * gc).astype(BF16)
                lhs2 = (theirs[i : i + rows, :].astype(F32) * rr2[...] * gc).astype(BF16)
                lhs = jnp.concatenate([lhs, lhs2], axis=1)
                v = jnp.dot(lhs, dpb[...], preferred_element_type=F32)
                put(v, slice(g * 896, (g + 1) * 896))
                i += count
            for g in range(len(OUT_TILES[p])):
                lhs = jnp.concatenate([mine[o : o + rows, :], theirs[o : o + rows, :]], axis=1)
                v = jnp.dot(lhs, cxb[...], preferred_element_type=F32)
                at = ni * 896 + g * OUT_W
                put(v, slice(at, at + OUT_W))
                o += count

    sources, others = operands
    adds = [v for p in range(3) for v, _ in extra[p]] if extra else []
    return call(
        kernel,
        [jax.ShapeDtypeStruct((rows, w), BF16) for w in widths(896)] * roles,
        (*sources, *others, *adds),
        [ANY] * 3 + [VM] * (6 + len(adds)),
        [VM] * 3 * roles,
        [pltpu.VMEM((total * 2, 256), BF16)] * 2
        + [
            pltpu.VMEM((total, 128), BF16),
            pltpu.VMEM((512, 896), BF16),
            pltpu.VMEM((512, OUT_W), BF16),
            pltpu.SemaphoreType.DMA((3,)),
        ],
        rows * 5 * 1536 * 1024 * roles,
        4_000_000 + rows * 40_000 * roles,
        24,
    )


def layer_kernel(tok, ctx, wout, out):
    for j in range(10):
        rows = pl.ds(j * 512, 512)
        v = lax.dot_general(ctx[...], wout[rows, :], NT, preferred_element_type=F32)
        out[:, rows] = (tok[:, rows].astype(F32) + v).astype(BF16)


def layer(tokens, context, wout):
    return call(
        layer_kernel,
        jax.ShapeDtypeStruct((256, 5120), BF16),
        (tokens, context, wout),
        [VM] * 3,
        VM,
        [],
        2_000_000_000,
        12_000_000,
        14,
    )


def input_kernel(cot, tok, rcol, dproj, win, out, val):
    r = rcol[...]
    total = jnp.zeros((256, 1), F32)
    for j in range(10):
        rows = pl.ds(j * 512, 512)
        dn = lax.dot_general(dproj[...], win[rows, 0:896], NT, preferred_element_type=F32)
        dn = dn * gain_row(win[rows, 896:1024])
        val[:, rows] = dn
        total = total + jnp.sum(tok[:, rows].astype(F32) * r * dn, axis=1, keepdims=True)
    mean = total / 5120.0
    for j in range(10):
        rows = pl.ds(j * 512, 512)
        v = r * (val[:, rows] - tok[:, rows].astype(F32) * r * mean)
        out[:, rows] = (cot[:, rows].astype(F32) + v).astype(BF16)


def input_side(cot, tok, rcol, dproj, win):
    return call(
        input_kernel,
        jax.ShapeDtypeStruct((256, 5120), BF16),
        (cot, tok, rcol, dproj, win),
        [VM] * 5,
        VM,
        [pltpu.VMEM((256, 5120), F32)],
        2_500_000_000,
        18_000_000,
        26,
    )


def first_join(corev, held, r1, q1, r2):
    def kernel(c, *refs):
        core = c[0]
        sems, ins, outs = refs[21], [], []
        for p in range(3):
            for i, at in enumerate((0, 16 + 32 * core, 48 - 32 * core, 32)):
                to = refs[18 + p].at[pl.ds(pl.multiple_of(at, 16), 16), :]
                ins.append(pltpu.make_async_copy(refs[p * 4 + i], to, sems.at[p * 6 + i]))
        for m in ins:
            m.start()
        for p in range(3):
            for m in ins[p * 4 : p * 4 + 4]:
                m.wait()
            whole = refs[18 + p]
            half = whole.at[pl.ds(pl.multiple_of(32 * core, 16), 32), :]
            outs.append(pltpu.make_async_copy(whole, refs[12 + p], sems.at[p * 6 + 4]))
            outs.append(pltpu.make_async_copy(half, refs[15 + p], sems.at[p * 6 + 5]))
            for m in outs[-2:]:
                m.start()
        for m in outs:
            m.wait()

    ins = [v for p in range(3) for v in (held[p], r1[p], q1[p], r2[p])]
    shapes = [jax.ShapeDtypeStruct((n, w), BF16) for n in (64, 32) for w in widths(IN_W)]
    scratch = [pltpu.VMEM((64, w), BF16) for w in widths(IN_W)] + [pltpu.SemaphoreType.DMA((18,))]
    out = call(kernel, shapes, (corev, *ins), [SM] + [ANY] * 12, [ANY] * 6, scratch, 1_000, 4_000_000, 60)
    return out[:3], out[3:]


def second_join(corev, held, r1, q1, r2, q2):
    def kernel(c, *refs):
        core = c[0]
        sems, outs = refs[24], []
        ins = []
        for p in range(3):
            whole = refs[21 + p]
            at = (0, 64 + 128 * core, 192 - 128 * core, 128 + 32 * core, 160 - 32 * core)
            for i in range(5):
                ref = refs[p * 5 + i]
                to = whole.at[pl.ds(pl.multiple_of(at[i], 16), ref.shape[0]), :]
                ins.append(pltpu.make_async_copy(ref, to, sems.at[p * 7 + i]))
        for m in ins:
            m.start()
        for p in range(3):
            for m in ins[p * 5 : p * 5 + 5]:
                m.wait()
            for i in range(2):
                at = 128 * core if i == 0 else 128 - 128 * core
                src = refs[21 + p].at[pl.ds(pl.multiple_of(at, 16), 128), :]
                m = pltpu.make_async_copy(src, refs[15 + i * 3 + p], sems.at[p * 7 + 5 + i])
                m.start()
                outs.append(m)
        for m in outs:
            m.wait()

    ins = [v for p in range(3) for v in (held[p], r1[p], q1[p], r2[p], q2[p])]
    shapes = [jax.ShapeDtypeStruct((128, w), BF16) for _ in range(2) for w in widths(IN_W)]
    scratch = [pltpu.VMEM((256, w), BF16) for w in widths(IN_W)] + [pltpu.SemaphoreType.DMA((21,))]
    out = call(kernel, shapes, (corev, *ins), [SM] + [ANY] * 15, [ANY] * 6, scratch, 1_000, 9_000_000, 60)
    return out[:3], out[3:]


def first_sum(corev, own, ra, qa):
    rows = (192, 128, 64)

    def kernel(c, *refs):
        core = c[0]
        work, held, sems = refs[18:21], refs[21:30], refs[30]
        ins, outs = [], []
        for p in range(3):
            for i in range(3):
                src = refs[p * 3 + i].at[pl.ds(0, rows[i]), :]
                ins.append(pltpu.make_async_copy(src, held[p * 3 + i], sems.at[p * 3 + i]))
        for m in ins:
            m.start()
        for p in range(3):
            for m in ins[p * 3 : p * 3 + 3]:
                m.wait()
            o, a, xa = held[p * 3 : p * 3 + 3]
            w = work[p]
            f = lambda ref, at: ref[at : at + 64, :].astype(F32)
            w[0:64, :] = (f(o, 0) + f(a, 0)).astype(BF16)
            w[64:128, :] = (f(o, 128) + f(xa, 0)).astype(BF16)
            w[128:192, :] = (f(o, 64) + f(a, 64)).astype(BF16)
            for i, (at, n) in enumerate(((64 * core, 64), (128, 64), (64 - 32 * core, 32))):
                src = w.at[pl.ds(pl.multiple_of(at, 16), n), :]
                m = pltpu.make_async_copy(src, refs[9 + i * 3 + p], sems.at[9 + p * 3 + i])
                m.start()
                outs.append(m)
        for m in outs:
            m.wait()

    ins = [v for p in range(3) for v in (own[p], ra[p], qa[p])]
    shapes = [jax.ShapeDtypeStruct((n, w), BF16) for n in (64, 64, 32) for w in widths(896)]
    scratch = [pltpu.VMEM((192, w), BF16) for w in widths(896)]
    scratch += [pltpu.VMEM((n, w), BF16) for w in widths(896) for n in rows]
    scratch += [pltpu.SemaphoreType.DMA((18,))]
    out = call(kernel, shapes, (corev, *ins), [SM] + [ANY] * 9, [ANY] * 9, scratch, 1_000, 9_000_000, 12)
    return out[:3], out[3:6], out[6:]


def second_sum(corev, zero, r1, q1, r2, q2):
    def kernel(c, *refs):
        core = c[0]
        for p in range(3):
            z, a, b, e, g = refs[p * 5 : p * 5 + 5]
            own, one, two, work = refs[15 + p], refs[18 + p], refs[21 + p], refs[24 + p]
            f = lambda ref: ref[...].astype(F32)
            work[...] = f(z) + f(a) + f(b)
            work[pl.ds(pl.multiple_of(32 * core, 16), 32), :] += f(e)
            work[pl.ds(pl.multiple_of(32 - 32 * core, 16), 32), :] += f(g)
            own[...] = work[0:16, :].astype(BF16)
            one[...] = work[pl.ds(pl.multiple_of(16 + 32 * core, 16), 16), :].astype(BF16)
            two[...] = work[32:48, :].astype(BF16)

    ins = [v for p in range(3) for v in (zero[p], r1[p], q1[p], r2[p], q2[p])]
    shapes = [jax.ShapeDtypeStruct((16, w), BF16) for _ in range(3) for w in widths(896)]
    scratch = [pltpu.VMEM((64, w), F32) for w in widths(896)]
    out = call(kernel, shapes, (corev, *ins), [SM] + [VM] * 15, [VM] * 9, scratch, 1_000, 4_000_000, 10)
    return out[:3], out[3:6], out[6:]


def each(function, *lists):
    return [function(p, *(v[p] for v in lists)) for p in range(3)]


def along(stage, step):
    return lambda p, value: move(value, ORDERS[p][stage], step)


def swapped(values):
    return [swap(v) for v in values]


def per_device(tokens, cotangent, in_weight, out_weight, norm_gain):
    core = lax.axis_index("dp") % 2
    first = core == 0
    mine = jnp.concatenate(
        [in_weight, jnp.broadcast_to(norm_gain[:, None], (40, 128)), out_weight], axis=1
    )
    other = swap(mine)
    chip = jnp.concatenate([jnp.where(first, mine, other), jnp.where(first, other, mine)], axis=0)
    held = []
    for ti, to in zip(IN_TILES, OUT_TILES):
        held.append(
            jnp.concatenate(
                [chip[t * 16 : t * 16 + 16, :IN_W] for t in ti]
                + [chip[t * 16 : t * 16 + 16, IN_W:] for t in to],
                axis=1,
            )
        )
    corev = core.astype(jnp.int32).reshape(1)
    table, other_table = chip_table(core), chip_table(1 - core)
    tie = lax.optimization_barrier
    r1 = each(along(0, 1), held)
    r2 = each(along(0, 2), held)
    held, half = first_join(corev, held, r1, swapped(r1), r2)
    late_tokens, _ = tie((tokens, held))
    x = late_tokens.astype(F32)
    rcol = lax.rsqrt(jnp.mean(x * x, axis=1, keepdims=True) + EPS)
    r1 = each(along(1, 1), held)
    r2 = each(along(1, 2), half)
    r2, rcol = tie((r2, rcol))
    rrow = rcol.reshape(1, 256)
    own_a, own_b = second_join(corev, held, r1, swapped(r1), r2, swapped(r2))
    got_a = each(along(2, 1), own_a)
    late_tokens, late_cot, _ = tie((tokens, cotangent, own_a))
    arranged = arrange(table, other_table, late_tokens, late_cot)
    got_a, arranged = tie((got_a, arranged))
    late_b, _ = tie((own_b, got_a))
    got_b = each(along(2, 1), late_b)
    lhs, lhs2 = arranged
    far = each(along(2, 1), got_a)
    swap_a = [tie((got_a[p], got_b[p]))[0] for p in range(3)]
    slots = [own_a, own_b, got_a, got_b, swapped(swap_a), swapped(got_b), far, swapped(far)]
    pieces = [slot[p] for p in range(3) for slot in slots]
    lhs2, rrow2, pieces = tie((lhs2, rrow, pieces))
    lhs2, rrow2 = swap(lhs2), swap(rrow2)

    context, dproj, gain, win, wout = core_call(table, tokens, rcol, cotangent, pieces)
    win, wout = win.reshape(5120, IN_W), wout.reshape(5120, OUT_W)
    context2, dproj2 = swap(context), swap(dproj)
    operands = (
        (lhs, lhs2, gain),
        (rrow, rrow2, dproj, dproj2, context, context2),
    )
    terms = grads(0, 128, operands, roles=2)
    far, near_b = terms[:3], terms[3:]
    got = each(along(2, -1), far)
    late_tokens, late_cot, _ = tie((tokens, cotangent, far))
    input_grad = input_side(late_cot, late_tokens, rcol, dproj, win)
    got, near_b, input_grad = tie((got, near_b, input_grad))
    rb = each(along(2, -1), near_b)
    near_a = grads(2, 128, operands, [[(got[p], 0)] for p in range(3)])
    ra = each(along(2, -1), near_a)
    operands, late_tokens, rb, _ = tie((operands, tokens, rb, near_a))
    qb = swapped(rb)
    own = grads(3, 192, operands, [[(qb[p], 0), (rb[p][:64], 128)] for p in range(3)])
    ra, own = tie((ra, own))
    zero, one, two = first_sum(corev, own, ra, swapped(ra))
    late_tokens, _ = tie((late_tokens, one))
    layer_out = layer(late_tokens, context, wout)
    r1 = each(along(1, -1), one)
    r2 = each(along(1, 2), two)
    r2, layer_out = tie((r2, layer_out))
    zero, one, two = second_sum(corev, zero, r1, swapped(r1), r2, swapped(r2))
    r1 = each(along(0, -1), one)
    r2 = each(along(0, 2), two)
    q1 = swapped(r1)
    f = lambda v: v.astype(F32)
    sums = [f(zero[p]) + f(r1[p]) + f(q1[p]) + f(r2[p]) for p in range(3)]
    scale = 1.0 / math.sqrt(32768.0)
    in_rows, out_rows = [], []
    for p in range(3):
        n = len(IN_TILES[p])
        in_rows += [sums[p][:, g * 896 : (g + 1) * 896] for g in range(n)]
        out_rows += [
            sums[p][:, n * 896 + g * OUT_W : n * 896 + (g + 1) * OUT_W] for g in range(len(OUT_TILES[p]))
        ]
    in_grad = lax.dynamic_slice_in_dim(jnp.concatenate(in_rows, axis=0), core * 40, 40, 0) * scale
    out_grad = lax.dynamic_slice_in_dim(jnp.concatenate(out_rows, axis=0), core * 40, 40, 0) * scale
    gain_grad = jnp.sum(in_weight.astype(F32) * in_grad, axis=1) / norm_gain.astype(F32)
    return layer_out, input_grad, in_grad, out_grad, gain_grad


def solution(mesh):
    rows = P(AXES, None)
    return jax.shard_map(
        per_device,
        mesh=mesh,
        in_specs=(rows, rows, rows, rows, P(AXES)),
        out_specs=(rows, rows, rows, rows, P(AXES)),
        check_vma=False,
    )
```

```python
import math

import jax
import jax.numpy as jnp
from jax import lax
from jax.experimental import pallas as pl
from jax.experimental.pallas import tpu as pltpu
from jax.sharding import PartitionSpec as P

HEAD_DIM = 128
HEADS = 5
EPS = 1e-06
AXES = ("blk", "dp")
F32 = jnp.float32
BF16 = jnp.bfloat16
ORDERS = ("xyz", "yzx", "zxy")
IN_TILES = ((0, 1), (2, 3), (4,))
OUT_TILES = ((0,), (1,), (2, 3, 4))
IN_W, OUT_W = 1024, 640
MIB = 1024 * 1024
NT = (((1,), (1,)), ((), ()))
TN = (((0,), (0,)), ((), ()))


def index_of(x, y, z, c):
    x, y, z = x % 4, y % 4, z % 4
    return ((y % 2) * 4 + x) * 16 + (y // 2) * 8 + z * 2 + c


def step_perm(axis, step):
    pairs = []
    for x in range(4):
        for y in range(4):
            for z in range(4):
                for c in range(2):
                    to = {"x": x, "y": y, "z": z}
                    to[axis] += step if c == 0 else -step
                    pairs.append((index_of(x, y, z, c), index_of(to["x"], to["y"], to["z"], c)))
    return pairs


def move(value, axis, step):
    return lax.ppermute(value, AXES, step_perm(axis, step))


def swap(value):
    return lax.ppermute(value, AXES, [(i, i ^ 1) for i in range(128)])


def chip_table(core):
    blk, dp = lax.axis_index("blk"), lax.axis_index("dp")
    here = {"x": blk % 4, "y": (dp // 8) * 2 + blk // 4, "z": (dp // 2) % 4}
    slot, u = lax.iota(jnp.int32, 64) // 8, lax.iota(jnp.int32, 64) % 8
    half = jnp.where((slot == 0) | (slot == 2) | (slot == 5) | (slot == 6), core, 1 - core)
    u = u + 8 * half
    received = (slot == 2) | (slot == 3)
    k3 = jnp.where(slot < 2, 0, jnp.where(slot >= 6, 2, jnp.where(received == (core == 0), 1, 3)))
    out = []
    for order in ORDERS:
        at = {a: (here[a] - k + 4) % 4 for a, k in zip(order, (u % 4, u // 4, k3))}
        out.append(((at["y"] % 2) * 4 + at["x"]) * 8 + (at["y"] // 2) * 4 + at["z"])
    return jnp.concatenate(out).astype(jnp.int32)


VM = pl.BlockSpec(memory_space=pltpu.VMEM)
SM = pl.BlockSpec(memory_space=pltpu.SMEM)
ANY = pl.BlockSpec(memory_space=pl.ANY)


def call(kernel, out_shape, ins, in_specs, out_specs, scratch, flops, nbytes, mib):
    return pl.pallas_call(
        kernel,
        out_shape=out_shape,
        in_specs=in_specs,
        out_specs=out_specs,
        scratch_shapes=scratch,
        compiler_params=pltpu.CompilerParams(vmem_limit_bytes=mib * MIB),
        cost_estimate=pl.CostEstimate(flops=flops, bytes_accessed=nbytes, transcendentals=0),
    )(*ins)


def gain_row(block):
    first = (lax.broadcasted_iota(jnp.int32, (8, 128), 1) == 0).astype(BF16)
    return lax.dot_general(first, block, NT, preferred_element_type=F32)[0:1]


def core_kernel(*refs):
    tbl, rcol, tok_in, cot_in = refs[:4]
    pieces = refs[4:28]
    ctx_ref, dproj_ref, gain_ref, win_out, wout_out = refs[28:33]
    held, (win, wout, tok, cot, acc, dacc, sems) = refs[33:36], refs[36:43]
    loads = [
        pltpu.make_async_copy(
            pieces[p * 8 + i], held[p].at[pl.ds(i * 128, 128), :], sems.at[p * 8 + i]
        )
        for p in range(3)
        for i in range(8)
    ]
    for c in loads:
        c.start()
    acts = [
        pltpu.make_async_copy(tok_in, tok, sems.at[24]),
        pltpu.make_async_copy(cot_in, cot, sems.at[25]),
    ]
    for c in acts:
        c.start()
    copies = []
    for p in range(3):
        ni = len(IN_TILES[p])
        for slot in range(8):
            loads[p * 8 + slot].wait()

            def place(u, _, p=p, ni=ni, slot=slot):
                src = pl.ds(pl.multiple_of(slot * 128 + u * 16, 16), 16)
                chip = tbl[p * 64 + slot * 8 + u]
                for g, t in enumerate(IN_TILES[p]):
                    win[chip, t * 16 : t * 16 + 16, :] = held[p][src, g * IN_W : (g + 1) * IN_W]
                for g, t in enumerate(OUT_TILES[p]):
                    at = ni * IN_W + g * OUT_W
                    wout[chip, t * 16 : t * 16 + 16, :] = held[p][src, at : at + OUT_W]
                return 0

            lax.fori_loop(0, 8, place, 0, unroll=4)
    for w, out in ((win, win_out), (wout, wout_out)):
        for i in range(2):
            chips = pl.ds(i * 32, 32)
            n = 26 + len(copies)
            copies.append(pltpu.make_async_copy(w.at[chips], out.at[chips], sems.at[n]))
            copies[-1].start()
    to = 0
    for first, count in ROLES:
        for p in range(3):
            for g in range(len(IN_TILES[p])):
                lanes = slice(g * IN_W + 896, (g + 1) * IN_W)
                gain_ref[to : to + count * 16, :] = held[p][first * 16 : (first + count) * 16, lanes]
                to += count * 16
    for c in acts:
        c.wait()
    r = rcol[...]
    for j in range(4):
        rows = pl.ds(j * 1280, 1280)
        chips = slice(j * 16, (j + 1) * 16)
        wi = win[chips].reshape(1280, IN_W)
        normed = (tok[:, rows].astype(F32) * r * gain_row(wi[:, 896:1024])).astype(BF16)
        term = jnp.dot(normed, wi[:, 0:896], preferred_element_type=F32)
        wo = wout[chips].reshape(1280, OUT_W)
        dterm = jnp.dot(cot[:, rows], wo, preferred_element_type=F32)
        if j == 0:
            acc[...] = term
            dacc[...] = dterm
        else:
            acc[...] += term
            dacc[...] += dterm
    factor = 1.0 / math.sqrt(HEAD_DIM)
    keys = acc[:, 640:768].astype(BF16)
    values = acc[:, 768:896].astype(BF16)
    causal = lax.broadcasted_iota(jnp.int32, (256, 256), 0) >= lax.broadcasted_iota(jnp.int32, (256, 256), 1)
    dk = jnp.zeros((256, 128), F32)
    dv = jnp.zeros((256, 128), F32)
    for h in range(HEADS):
        cols = slice(h * 128, (h + 1) * 128)
        q = acc[:, cols].astype(BF16)
        dc = dacc[:, cols].astype(BF16)
        s = lax.dot_general(q, keys, NT, preferred_element_type=F32) * factor
        s = jnp.where(causal, s, -jnp.inf)
        e = jnp.exp(s - jnp.max(s, axis=1, keepdims=True))
        wf = e / jnp.sum(e, axis=1, keepdims=True)
        wb = wf.astype(BF16)
        ctx_ref[:, cols] = jnp.dot(wb, values, preferred_element_type=F32).astype(BF16)
        dw = lax.dot_general(dc, values, NT, preferred_element_type=F32)
        ds = (wf * (dw - jnp.sum(wf * dw, axis=1, keepdims=True))).astype(BF16)
        dq = jnp.dot(ds, keys, preferred_element_type=F32) * factor
        dproj_ref[:, cols] = dq.astype(BF16)
        dk = dk + lax.dot_general(ds, q, TN, preferred_element_type=F32)
        dv = dv + lax.dot_general(wb, dc, TN, preferred_element_type=F32)
    dproj_ref[:, 640:768] = (dk * factor).astype(BF16)
    dproj_ref[:, 768:896] = dv.astype(BF16)
    for c in copies:
        c.wait()


def widths(in_w):
    return [len(a) * in_w + len(b) * OUT_W for a, b in zip(IN_TILES, OUT_TILES)]


def core_call(table, tokens, rcol, cotangent, pieces):
    return call(
        core_kernel,
        (
            jax.ShapeDtypeStruct((256, 640), BF16),
            jax.ShapeDtypeStruct((256, 896), BF16),
            jax.ShapeDtypeStruct((3200, 128), BF16),
            jax.ShapeDtypeStruct((64, 80, IN_W), BF16),
            jax.ShapeDtypeStruct((64, 80, OUT_W), BF16),
        ),
        (table, rcol, tokens, cotangent, *pieces),
        [SM, VM] + [ANY] * 26,
        [VM] * 3 + [ANY] * 2,
        [pltpu.VMEM((1024, w), BF16) for w in widths(IN_W)]
        + [
            pltpu.VMEM((64, 80, IN_W), BF16),
            pltpu.VMEM((64, 80, OUT_W), BF16),
            pltpu.VMEM((256, 5120), BF16),
            pltpu.VMEM((256, 5120), BF16),
            pltpu.VMEM((256, 896), F32),
            pltpu.VMEM((256, 640), F32),
            pltpu.SemaphoreType.DMA((32,)),
        ],
        4_500_000_000,
        40_000_000,
        60,
    )


ROLES = ((48, 8), (24, 8), (16, 8), (0, 16))


def arrange_kernel(tbl, tbl2, tok, cot, own, other, tt, ct):
    def turn(j, _):
        at = pl.multiple_of(j * 128, 128)
        tt[pl.ds(at, 128), :] = tok[:, pl.ds(at, 128)].T
        ct[pl.ds(at, 128), :] = cot[:, pl.ds(at, 128)].T
        return 0

    lax.fori_loop(0, 40, turn, 0, unroll=2)
    for table, out in ((tbl, own), (tbl2, other)):
        at = 0
        for first, count in ROLES:
            for source, tiles in ((tt, IN_TILES), (ct, OUT_TILES)):
                for p in range(3):
                    for t in tiles[p]:

                        def unit(u, _, p=p, t=t, first=first, at=at, table=table, out=out, source=source):
                            row = table[p * 64 + first + u] * 80 + t * 16
                            src = pl.ds(pl.multiple_of(row, 16), 16)
                            out[pl.ds(pl.multiple_of(at + u * 16, 16), 16), :] = source[src, :]
                            return 0

                        lax.fori_loop(0, count, unit, 0, unroll=8)
                        at += count * 16


def arrange(table, other, tokens, cotangent):
    return call(
        arrange_kernel,
        (jax.ShapeDtypeStruct((6400, 256), BF16),) * 2,
        (table, other, tokens, cotangent),
        [SM] * 2 + [VM] * 2,
        [VM] * 2,
        [pltpu.VMEM((5120, 256), BF16)] * 2,
        1_000_000,
        12_000_000,
        22,
    )


def grads(role, rows, operands, extra=(), roles=1):
    count = ROLES[role][1] * 16
    first = sum(c * 16 * 5 for _, c in ROLES[:role])
    total = count * 5 * roles
    n_extra = len(extra[0]) if extra else 0
    plan = [(v.shape[0], at) for v, at in extra[0]] if extra else []

    def kernel(*refs):
        sources, (rr, rr2, dp, dp2, cx, cx2) = refs[:3], refs[3:9]
        adds = refs[9 : 9 + 3 * n_extra]
        outs = refs[9 + 3 * n_extra : 9 + 3 * (n_extra + roles)]
        mine, theirs, gain, dpb, cxb, sems = refs[9 + 3 * (n_extra + roles) :]
        loads = [
            pltpu.make_async_copy(src.at[pl.ds(first * n, total * n), :], to, sems.at[i])
            for i, (src, to, n) in enumerate(zip(sources, (mine, theirs, gain), (2, 2, 1)))
        ]
        for c in loads:
            c.start()
        dpb[0:256, :] = dp[...]
        dpb[256:512, :] = dp2[...]
        cxb[0:256, :] = cx[...]
        cxb[256:512, :] = cx2[...]
        for c in loads:
            c.wait()
        used = 0
        for q in range(3 * roles):
            p = q % 3
            if p == 0:
                i = q // 3 * count * 10
                o = i + count * 5
            ni = len(IN_TILES[p])

            def put(v, lanes, p=p, q=q):
                for k, (n, at) in enumerate(plan):
                    more = adds[p * n_extra + k][:, lanes].astype(F32)
                    parts = [v[:at]] if at else []
                    parts.append(v[at : at + n] + more)
                    if at + n < rows:
                        parts.append(v[at + n :])
                    v = parts[0] if len(parts) == 1 else jnp.concatenate(parts, axis=0)
                outs[q][:, lanes] = v.astype(BF16)

            for g in range(ni):
                gc = gain[used : used + rows, :].astype(F32)[:, 0:1]
                used += count
                lhs = (mine[i : i + rows, :].astype(F32) * rr[...] * gc).astype(BF16)
                lhs2 = (theirs[i : i + rows, :].astype(F32) * rr2[...] * gc).astype(BF16)
                lhs = jnp.concatenate([lhs, lhs2], axis=1)
                v = jnp.dot(lhs, dpb[...], preferred_element_type=F32)
                put(v, slice(g * 896, (g + 1) * 896))
                i += count
            for g in range(len(OUT_TILES[p])):
                lhs = jnp.concatenate([mine[o : o + rows, :], theirs[o : o + rows, :]], axis=1)
                v = jnp.dot(lhs, cxb[...], preferred_element_type=F32)
                at = ni * 896 + g * OUT_W
                put(v, slice(at, at + OUT_W))
                o += count

    sources, others = operands
    adds = [v for p in range(3) for v, _ in extra[p]] if extra else []
    return call(
        kernel,
        [jax.ShapeDtypeStruct((rows, w), BF16) for w in widths(896)] * roles,
        (*sources, *others, *adds),
        [ANY] * 3 + [VM] * (6 + len(adds)),
        [VM] * 3 * roles,
        [pltpu.VMEM((total * 2, 256), BF16)] * 2
        + [
            pltpu.VMEM((total, 128), BF16),
            pltpu.VMEM((512, 896), BF16),
            pltpu.VMEM((512, OUT_W), BF16),
            pltpu.SemaphoreType.DMA((3,)),
        ],
        rows * 5 * 1536 * 1024 * roles,
        4_000_000 + rows * 40_000 * roles,
        24,
    )


def layer_kernel(tok, ctx, wout, out):
    for j in range(10):
        rows = pl.ds(j * 512, 512)
        v = lax.dot_general(ctx[...], wout[rows, :], NT, preferred_element_type=F32)
        out[:, rows] = (tok[:, rows].astype(F32) + v).astype(BF16)


def layer(tokens, context, wout):
    return call(
        layer_kernel,
        jax.ShapeDtypeStruct((256, 5120), BF16),
        (tokens, context, wout),
        [VM] * 3,
        VM,
        [],
        2_000_000_000,
        12_000_000,
        14,
    )


def input_kernel(cot, tok, rcol, dproj, win, out, val):
    r = rcol[...]
    total = jnp.zeros((256, 1), F32)
    for j in range(10):
        rows = pl.ds(j * 512, 512)
        dn = lax.dot_general(dproj[...], win[rows, 0:896], NT, preferred_element_type=F32)
        dn = dn * gain_row(win[rows, 896:1024])
        val[:, rows] = dn
        total = total + jnp.sum(tok[:, rows].astype(F32) * r * dn, axis=1, keepdims=True)
    mean = total / 5120.0
    for j in range(10):
        rows = pl.ds(j * 512, 512)
        v = r * (val[:, rows] - tok[:, rows].astype(F32) * r * mean)
        out[:, rows] = (cot[:, rows].astype(F32) + v).astype(BF16)


def input_side(cot, tok, rcol, dproj, win):
    return call(
        input_kernel,
        jax.ShapeDtypeStruct((256, 5120), BF16),
        (cot, tok, rcol, dproj, win),
        [VM] * 5,
        VM,
        [pltpu.VMEM((256, 5120), F32)],
        2_500_000_000,
        18_000_000,
        26,
    )


def first_join(corev, held, r1, q1, r2):
    def kernel(c, *refs):
        core = c[0]
        sems, ins, outs = refs[21], [], []
        for p in range(3):
            for i, at in enumerate((0, 16 + 32 * core, 48 - 32 * core, 32)):
                to = refs[18 + p].at[pl.ds(pl.multiple_of(at, 16), 16), :]
                ins.append(pltpu.make_async_copy(refs[p * 4 + i], to, sems.at[p * 6 + i]))
        for m in ins:
            m.start()
        for p in range(3):
            for m in ins[p * 4 : p * 4 + 4]:
                m.wait()
            whole = refs[18 + p]
            half = whole.at[pl.ds(pl.multiple_of(32 * core, 16), 32), :]
            outs.append(pltpu.make_async_copy(whole, refs[12 + p], sems.at[p * 6 + 4]))
            outs.append(pltpu.make_async_copy(half, refs[15 + p], sems.at[p * 6 + 5]))
            for m in outs[-2:]:
                m.start()
        for m in outs:
            m.wait()

    ins = [v for p in range(3) for v in (held[p], r1[p], q1[p], r2[p])]
    shapes = [jax.ShapeDtypeStruct((n, w), BF16) for n in (64, 32) for w in widths(IN_W)]
    scratch = [pltpu.VMEM((64, w), BF16) for w in widths(IN_W)] + [pltpu.SemaphoreType.DMA((18,))]
    out = call(kernel, shapes, (corev, *ins), [SM] + [ANY] * 12, [ANY] * 6, scratch, 1_000, 4_000_000, 60)
    return out[:3], out[3:]


def second_join(corev, held, r1, q1, r2, q2):
    def kernel(c, *refs):
        core = c[0]
        sems, outs = refs[24], []
        ins = []
        for p in range(3):
            whole = refs[21 + p]
            at = (0, 64 + 128 * core, 192 - 128 * core, 128 + 32 * core, 160 - 32 * core)
            for i in range(5):
                ref = refs[p * 5 + i]
                to = whole.at[pl.ds(pl.multiple_of(at[i], 16), ref.shape[0]), :]
                ins.append(pltpu.make_async_copy(ref, to, sems.at[p * 7 + i]))
        for m in ins:
            m.start()
        for p in range(3):
            for m in ins[p * 5 : p * 5 + 5]:
                m.wait()
            for i in range(2):
                at = 128 * core if i == 0 else 128 - 128 * core
                src = refs[21 + p].at[pl.ds(pl.multiple_of(at, 16), 128), :]
                m = pltpu.make_async_copy(src, refs[15 + i * 3 + p], sems.at[p * 7 + 5 + i])
                m.start()
                outs.append(m)
        for m in outs:
            m.wait()

    ins = [v for p in range(3) for v in (held[p], r1[p], q1[p], r2[p], q2[p])]
    shapes = [jax.ShapeDtypeStruct((128, w), BF16) for _ in range(2) for w in widths(IN_W)]
    scratch = [pltpu.VMEM((256, w), BF16) for w in widths(IN_W)] + [pltpu.SemaphoreType.DMA((21,))]
    out = call(kernel, shapes, (corev, *ins), [SM] + [ANY] * 15, [ANY] * 6, scratch, 1_000, 9_000_000, 60)
    return out[:3], out[3:]


def first_sum(corev, own, ra, qa):
    rows = (192, 128, 64)

    def kernel(c, *refs):
        core = c[0]
        work, held, sems = refs[18:21], refs[21:30], refs[30]
        ins, outs = [], []
        for p in range(3):
            for i in range(3):
                src = refs[p * 3 + i].at[pl.ds(0, rows[i]), :]
                ins.append(pltpu.make_async_copy(src, held[p * 3 + i], sems.at[p * 3 + i]))
        for m in ins:
            m.start()
        for p in range(3):
            for m in ins[p * 3 : p * 3 + 3]:
                m.wait()
            o, a, xa = held[p * 3 : p * 3 + 3]
            w = work[p]
            f = lambda ref, at: ref[at : at + 64, :].astype(F32)
            w[0:64, :] = (f(o, 0) + f(a, 0)).astype(BF16)
            w[64:128, :] = (f(o, 128) + f(xa, 0)).astype(BF16)
            w[128:192, :] = (f(o, 64) + f(a, 64)).astype(BF16)
            for i, (at, n) in enumerate(((64 * core, 64), (128, 64), (64 - 32 * core, 32))):
                src = w.at[pl.ds(pl.multiple_of(at, 16), n), :]
                m = pltpu.make_async_copy(src, refs[9 + i * 3 + p], sems.at[9 + p * 3 + i])
                m.start()
                outs.append(m)
        for m in outs:
            m.wait()

    ins = [v for p in range(3) for v in (own[p], ra[p], qa[p])]
    shapes = [jax.ShapeDtypeStruct((n, w), BF16) for n in (64, 64, 32) for w in widths(896)]
    scratch = [pltpu.VMEM((192, w), BF16) for w in widths(896)]
    scratch += [pltpu.VMEM((n, w), BF16) for w in widths(896) for n in rows]
    scratch += [pltpu.SemaphoreType.DMA((18,))]
    out = call(kernel, shapes, (corev, *ins), [SM] + [ANY] * 9, [ANY] * 9, scratch, 1_000, 9_000_000, 12)
    return out[:3], out[3:6], out[6:]


def second_sum(corev, zero, r1, q1, r2, q2):
    def kernel(c, *refs):
        core = c[0]
        for p in range(3):
            z, a, b, e, g = refs[p * 5 : p * 5 + 5]
            own, one, two, work = refs[15 + p], refs[18 + p], refs[21 + p], refs[24 + p]
            f = lambda ref: ref[...].astype(F32)
            work[...] = f(z) + f(a) + f(b)
            work[pl.ds(pl.multiple_of(32 * core, 16), 32), :] += f(e)
            work[pl.ds(pl.multiple_of(32 - 32 * core, 16), 32), :] += f(g)
            own[...] = work[0:16, :].astype(BF16)
            one[...] = work[pl.ds(pl.multiple_of(16 + 32 * core, 16), 16), :].astype(BF16)
            two[...] = work[32:48, :].astype(BF16)

    ins = [v for p in range(3) for v in (zero[p], r1[p], q1[p], r2[p], q2[p])]
    shapes = [jax.ShapeDtypeStruct((16, w), BF16) for _ in range(3) for w in widths(896)]
    scratch = [pltpu.VMEM((64, w), F32) for w in widths(896)]
    out = call(kernel, shapes, (corev, *ins), [SM] + [VM] * 15, [VM] * 9, scratch, 1_000, 4_000_000, 10)
    return out[:3], out[3:6], out[6:]


def each(function, *lists):
    return [function(p, *(v[p] for v in lists)) for p in range(3)]


def along(stage, step):
    return lambda p, value: move(value, ORDERS[p][stage], step)


def swapped(values):
    return [swap(v) for v in values]


def per_device(tokens, cotangent, in_weight, out_weight, norm_gain):
    core = lax.axis_index("dp") % 2
    first = core == 0
    mine = jnp.concatenate(
        [in_weight, jnp.broadcast_to(norm_gain[:, None], (40, 128)), out_weight], axis=1
    )
    other = swap(mine)
    chip = jnp.concatenate([jnp.where(first, mine, other), jnp.where(first, other, mine)], axis=0)
    held = []
    for ti, to in zip(IN_TILES, OUT_TILES):
        held.append(
            jnp.concatenate(
                [chip[t * 16 : t * 16 + 16, :IN_W] for t in ti]
                + [chip[t * 16 : t * 16 + 16, IN_W:] for t in to],
                axis=1,
            )
        )
    corev = core.astype(jnp.int32).reshape(1)
    table, other_table = chip_table(core), chip_table(1 - core)
    tie = lax.optimization_barrier
    r1 = each(along(0, 1), held)
    r2 = each(along(0, 2), held)
    held, half = first_join(corev, held, r1, swapped(r1), r2)
    late_tokens, _ = tie((tokens, held))
    x = late_tokens.astype(F32)
    rcol = lax.rsqrt(jnp.mean(x * x, axis=1, keepdims=True) + EPS)
    r1 = each(along(1, 1), held)
    r2 = each(along(1, 2), half)
    r2, rcol = tie((r2, rcol))
    rrow = rcol.reshape(1, 256)
    own_a, own_b = second_join(corev, held, r1, swapped(r1), r2, swapped(r2))
    got_a = each(along(2, 1), own_a)
    late_tokens, late_cot, _ = tie((tokens, cotangent, own_a))
    arranged = arrange(table, other_table, late_tokens, late_cot)
    got_a, arranged = tie((got_a, arranged))
    lhs, lhs2 = arranged
    far = each(along(2, 1), got_a)
    other_a = swapped(got_a)
    late_b = [tie((own_b[p], other_a[p]))[0] for p in range(3)]
    got_b = each(along(2, 1), late_b)
    slots = [own_a, own_b, got_a, got_b, other_a, swapped(got_b), far, swapped(far)]
    pieces = [slot[p] for p in range(3) for slot in slots]
    lhs2, rrow2, pieces = tie((lhs2, rrow, pieces))
    lhs2, rrow2 = swap(lhs2), swap(rrow2)

    context, dproj, gain, win, wout = core_call(table, tokens, rcol, cotangent, pieces)
    win, wout = win.reshape(5120, IN_W), wout.reshape(5120, OUT_W)
    context2, dproj2 = swap(context), swap(dproj)
    operands = (
        (lhs, lhs2, gain),
        (rrow, rrow2, dproj, dproj2, context, context2),
    )
    terms = grads(0, 128, operands, roles=2)
    far, near_b = terms[:3], terms[3:]
    got = each(along(2, -1), far)
    late_tokens, late_cot, _ = tie((tokens, cotangent, far))
    input_grad = input_side(late_cot, late_tokens, rcol, dproj, win)
    got, near_b, input_grad = tie((got, near_b, input_grad))
    rb = each(along(2, -1), near_b)
    near_a = grads(2, 128, operands, [[(got[p], 0)] for p in range(3)])
    ra = each(along(2, -1), near_a)
    operands, late_tokens, rb, _ = tie((operands, tokens, rb, near_a))
    qb = swapped(rb)
    own = grads(3, 192, operands, [[(qb[p], 0), (rb[p][:64], 128)] for p in range(3)])
    ra, own = tie((ra, own))
    zero, one, two = first_sum(corev, own, ra, swapped(ra))
    late_tokens, _ = tie((late_tokens, one))
    layer_out = layer(late_tokens, context, wout)
    r1 = each(along(1, -1), one)
    r2 = each(along(1, 2), two)
    r2, layer_out = tie((r2, layer_out))
    zero, one, two = second_sum(corev, zero, r1, swapped(r1), r2, swapped(r2))
    r1 = each(along(0, -1), one)
    r2 = each(along(0, 2), two)
    q1 = swapped(r1)
    f = lambda v: v.astype(F32)
    sums = [f(zero[p]) + f(r1[p]) + f(q1[p]) + f(r2[p]) for p in range(3)]
    scale = 1.0 / math.sqrt(32768.0)
    in_rows, out_rows = [], []
    for p in range(3):
        n = len(IN_TILES[p])
        in_rows += [sums[p][:, g * 896 : (g + 1) * 896] for g in range(n)]
        out_rows += [
            sums[p][:, n * 896 + g * OUT_W : n * 896 + (g + 1) * OUT_W] for g in range(len(OUT_TILES[p]))
        ]
    in_grad = lax.dynamic_slice_in_dim(jnp.concatenate(in_rows, axis=0), core * 40, 40, 0) * scale
    out_grad = lax.dynamic_slice_in_dim(jnp.concatenate(out_rows, axis=0), core * 40, 40, 0) * scale
    gain_grad = jnp.sum(in_weight.astype(F32) * in_grad, axis=1) / norm_gain.astype(F32)
    return layer_out, input_grad, in_grad, out_grad, gain_grad


def solution(mesh):
    rows = P(AXES, None)
    return jax.shard_map(
        per_device,
        mesh=mesh,
        in_specs=(rows, rows, rows, rows, P(AXES)),
        out_specs=(rows, rows, rows, rows, P(AXES)),
        check_vma=False,
    )
```
